32 devices in a mesh: rows: 32 (over z, y, x, core), cols: 1.
Axes of the slice: x: 2, y: 2, z: 4, core: 2. Of those that a mesh axis runs over, the one named last changes fastest.
Arguments:
- slab: bfloat16 [4096, 4096], P('rows', 'cols'), may hold values from -6 to 6
- cross: bfloat16 [4096, 128], P('rows', 'cols'), may hold values from 0 to 6, as said below
- obs_index: int32 [128], replicated, may hold values from 0 to 4095, as said below
- noise: float32 [128], replicated, may hold values from 0.25 to 2
Outputs:
- posterior: bfloat16 [4096, 4096], P('rows', 'cols')
The draws below stay inside these ranges and needn't reach their ends.
Inputs may be any that keep to these rules, and one draw needn't show every extreme that they name: `obs_index`: the 128 segments are distinct. Split the segments into blocks of 128 in order: a quarter of the blocks hold exactly 12 inspected segments, a quarter hold 4, the rest none. `cross`: innovation is positive definite.
All inputs are finite; a program needn't handle non-finite values.
Results may differ from the reference program's by a relative error of at most 0.0099.
Values may be sent and summed in bfloat16 or wider, within the bound.
No kernel may reach another device: no remote copies, remote signals or barrier semaphores. Data moves between devices by JAX's collectives and lax.ppermute only.
A program may use at most 64 MiB of HBM per device.

```python
import math
import jax
import jax.numpy as jnp
from jax import lax

ROWS_DEV = 128
OBS_DEV = 4
W = 4096
SEGMENTS = 4096
M = 128
CAP = 12


def inspection_layout(key):
    base = jax.random.fold_in(key, 11)
    key_owner = jax.random.fold_in(base, 1)
    key_rows = jax.random.fold_in(base, 2)
    key_order = jax.random.fold_in(base, 3)
    groups = SEGMENTS // ROWS_DEV
    owner_perm = jax.random.permutation(key_owner, groups).astype(jnp.int32)
    position = jnp.arange(groups, dtype=jnp.int32) % 4
    by_position = jnp.where(position == 0, CAP, jnp.where(position == 1, OBS_DEV, 0)).astype(jnp.int32)
    counts = jnp.zeros((groups,), jnp.int32).at[owner_perm].set(by_position)
    row_keys = jax.random.split(key_rows, groups)
    row_perms = jax.vmap(lambda k: jax.random.permutation(k, ROWS_DEV))(row_keys).astype(jnp.int32)
    starts = (jnp.arange(groups, dtype=jnp.int32) * ROWS_DEV)[:, None]
    candidates = row_perms[:, :CAP] + starts
    valid = jnp.arange(CAP, dtype=jnp.int32)[None, :] < counts[:, None]
    flat_cand = candidates.reshape(-1)
    flat_flag = jnp.where(valid.reshape(-1), 0, 1).astype(jnp.int32)
    order = jnp.argsort(flat_flag, stable=True)
    chosen = flat_cand[order][:M]
    shuffle = jax.random.permutation(key_order, M).astype(jnp.int32)
    return chosen[shuffle].astype(jnp.int32)


def draw_obs_index(key, part):
    return inspection_layout(key)


def draw_cross(key, part):
    chosen = inspection_layout(key)
    float_key = jax.random.fold_in(key, 5)
    key_scale = jax.random.fold_in(float_key, 1)
    key_nugget = jax.random.fold_in(float_key, 2)
    key_class = jax.random.fold_in(float_key, 3)
    class_count = max(M // 2, 1)
    lot_class = jax.random.randint(key_class, (SEGMENTS,), 0, class_count).astype(jnp.int32)
    variance = jnp.exp(jax.random.uniform(key_scale, (SEGMENTS,), jnp.float32, 0.0, jnp.log(4.0)))
    broad_length = 4.0 * ROWS_DEV
    nugget = jax.random.uniform(key_nugget, (M,), jnp.float32, 0.5, 1.0)
    spread = jnp.sqrt(variance)
    positions = jnp.arange(SEGMENTS, dtype=jnp.int32)
    distance = jnp.abs(positions[:, None] - chosen[None, :]).astype(jnp.float32)
    local_part = jnp.exp(-distance / (8.0 * ROWS_DEV))
    ratio = distance / broad_length
    broad_part = jnp.exp(-ratio * ratio)
    same_lot = (lot_class[:, None] == lot_class[chosen][None, :]).astype(jnp.float32)
    kernel = spread[:, None] * spread[chosen][None, :] * (0.4 * local_part + 0.2 * broad_part + 0.4 * same_lot)
    on_point = positions[:, None] == chosen[None, :]
    entries = kernel + jnp.where(on_point, nugget[None, :], 0.0)
    return entries.astype(jnp.bfloat16)


def levels(rng, shape, shards, low, largest):
    level, own = 1.0, jax.random.fold_in(rng, 6)
    for dim, parts in shards:
        draws = jnp.exp(jax.random.uniform(jax.random.fold_in(own, dim), (parts,), jnp.float32, low / len(shards), largest / len(shards)))
        level = level * jnp.repeat(draws, shape[dim] // parts).reshape([-1 if axis == dim else 1 for axis in range(len(shape))])
    return level


def scatter_about(own_key, dims, deviation, reach, cuts=(), kind=jnp.bfloat16):
    values = deviation * jax.random.normal(own_key, dims, jnp.float32)
    if cuts:
        values = values * levels(own_key, dims, cuts, -0.22, 0.18)
    return jnp.clip(values, -reach, reach).astype(kind)


def setup_inputs(seed: int = 0) -> dict:
    key_of = jax.random.split(jax.random.key(seed), 5)
    slab = scatter_about(key_of[0], (SEGMENTS, W), 1.0, 6.0, ((0, 32),))
    cross = draw_cross(jax.random.fold_in(key_of[4], 71), 0)
    obs_index = draw_obs_index(jax.random.fold_in(key_of[4], 71), 0)
    noise = jnp.clip(jnp.exp(jax.random.uniform(key_of[3], (M,), jnp.float32, math.log(0.25), math.log(2.0))), 0.25, 2.0)
    return dict(slab=slab, cross=cross, obs_index=obs_index, noise=noise)


def solve_gain(factor, right_side):
    forward = lax.linalg.triangular_solve(factor, right_side, left_side=True, lower=True)
    return lax.linalg.triangular_solve(factor, forward, left_side=True, lower=True, transpose_a=True)

def reference(slab, cross, obs_index, noise):
    picked = cross[obs_index].astype(jnp.float32)
    innovation = 0.5 * (picked + picked.T) + jnp.diag(noise.astype(jnp.float32))
    factor = jnp.linalg.cholesky(innovation)
    observed = slab[obs_index].astype(jnp.float32)
    gain = solve_gain(factor, observed).astype(jnp.bfloat16)
    slab_blocks = slab.reshape(SEGMENTS // ROWS_DEV, ROWS_DEV, W)
    cross_blocks = cross.reshape(SEGMENTS // ROWS_DEV, ROWS_DEV, M)

    def update_block(pair):
        slab_part, cross_part = pair
        product = jnp.dot(cross_part.astype(jnp.float32), gain.astype(jnp.float32), preferred_element_type=jnp.float32)
        return (slab_part.astype(jnp.float32) - product).astype(jnp.bfloat16)
    result = lax.map(update_block, (slab_blocks, cross_blocks))
    return result.reshape(SEGMENTS, W)
```

```python
import functools

import jax
import jax.numpy as jnp
from jax import lax
from jax.experimental import pallas as pl
from jax.experimental.pallas import tpu as pltpu
from jax.sharding import PartitionSpec as P

CAP = 12
SLOTS = 16
PLANE = 8
VMEM = pl.BlockSpec(memory_space=pltpu.VMEM)


def dot32(a, b):
    return jnp.dot(a, b, preferred_element_type=jnp.float32)


def solve_gain(factor, right_side):
    forward = lax.linalg.triangular_solve(factor, right_side, left_side=True, lower=True)
    return lax.linalg.triangular_solve(
        factor, forward, left_side=True, lower=True, transpose_a=True
    )


def make_factor(picked_half, noise):
    picked = lax.all_gather(picked_half, "cols", axis=1, tiled=True).astype(jnp.float32)
    innovation = 0.5 * (picked + picked.T) + jnp.diag(noise)
    return jnp.linalg.cholesky(innovation)


def general_body(slab, cross, obs_index, noise):
    row_count = slab.shape[0]
    groups = lax.axis_size("rows")
    owners = obs_index // row_count
    local_row = obs_index % row_count
    owner_hit = (owners[:, None] == jnp.arange(groups, dtype=jnp.int32)[None, :]).astype(jnp.int32)
    before = jnp.cumsum(owner_hit, axis=0) - owner_hit
    slot_rank = jnp.sum(before * owner_hit, axis=1)
    mine = owners == lax.axis_index("rows")
    slot_hit = (
        mine[:, None] & (slot_rank[:, None] == jnp.arange(CAP, dtype=jnp.int32)[None, :])
    ).astype(jnp.bfloat16)
    row_hit = (local_row[:, None] == jnp.arange(row_count, dtype=jnp.int32)[None, :]).astype(
        jnp.bfloat16
    )
    selector = dot32(slot_hit.T, row_hit).astype(jnp.bfloat16)
    packed_cross = dot32(selector, cross).astype(jnp.bfloat16)
    packed_slab = dot32(selector, slab).astype(jnp.bfloat16)
    placed = owners * CAP + slot_rank
    all_cross, all_slab = (
        lax.all_gather(packed_cross, "rows", axis=0, tiled=True),
        lax.all_gather(packed_slab, "rows", axis=0, tiled=True),
    )
    factor = make_factor(all_cross[placed], noise)
    observed = all_slab[placed].astype(jnp.float32)
    gain = solve_gain(factor, observed).astype(jnp.bfloat16)
    update = dot32(lax.all_gather(cross, "cols", axis=1, tiled=True), gain)
    return (slab.astype(jnp.float32) - update).astype(jnp.bfloat16)


def spread_index(obs_ref, rows):
    count = obs_ref.shape[1]
    along = jnp.broadcast_to(obs_ref[...], (count, count))
    down = along.astype(jnp.float32).T.astype(jnp.int32)
    earlier_row = lax.broadcasted_iota(jnp.int32, (count, count), 0)
    earlier_col = lax.broadcasted_iota(jnp.int32, (count, count), 1)
    same = along // rows == down // rows
    rank_along = jnp.sum(
        jnp.where(same & (earlier_row < earlier_col), 1.0, 0.0), axis=0, keepdims=True
    ).astype(jnp.int32)
    rank_down = jnp.sum(
        jnp.where(same & (earlier_col < earlier_row), 1.0, 0.0), axis=1, keepdims=True
    ).astype(jnp.int32)
    return along, down, rank_along, rank_down


def pick_kernel(groups, width, obs_ref, slab_ref, cross_ref, out_ref):
    rows, count = slab_ref.shape[0], obs_ref.shape[1]
    me = lax.axis_index("rows")
    along, down, rank, _ = spread_index(obs_ref, rows)
    picks = 4 * SLOTS
    slot = lax.broadcasted_iota(jnp.int32, (picks, count), 0)
    within, part = slot % SLOTS, slot // SLOTS
    wanted = jnp.where(
        part == 0,
        jnp.where(within < CAP, within, -1),
        jnp.where(within >= CAP, 4 * (part - 1) + within - CAP, -1),
    )
    mine = (along[:1] // rows) == me
    hit = jnp.where(mine & (rank == wanted), 1.0, 0.0).astype(jnp.bfloat16)
    local = lax.broadcasted_iota(jnp.int32, (count, rows), 1) == down[:, :rows] % rows
    selector = dot32(hit, jnp.where(local, 1.0, 0.0).astype(jnp.bfloat16)).astype(jnp.bfloat16)
    cross_part = dot32(selector[:SLOTS], cross_ref[...]).astype(jnp.bfloat16)
    lanes = width // 4
    for group in range(PLANE):
        got = dot32(selector, slab_ref[:, group * width : (group + 1) * width])
        tail = got[:, 3 * lanes :]
        block = jnp.concatenate(
            [
                (
                    got[:SLOTS, t * lanes : (t + 1) * lanes]
                    + tail[(t + 1) * SLOTS : (t + 2) * SLOTS]
                ).astype(jnp.bfloat16)
                for t in range(3)
            ]
            + [cross_part],
            axis=1,
        )
        for level in range(groups // PLANE):
            at = (level * PLANE + group) * SLOTS
            out_ref[at : at + SLOTS, :] = block


def compact_kernel(rows, obs_ref, noise_ref, got_ref, a_ref, b_ref, inn_ref):
    count, slots = obs_ref.shape[1], got_ref.shape[0]
    lanes = got_ref.shape[1] // 4
    _, down, _, rank = spread_index(obs_ref, rows)
    owner = down[:, :1] // rows
    lane = lax.broadcasted_iota(jnp.int32, (count, slots), 1)
    within = lane % SLOTS
    owned = owner == lane // SLOTS

    def one_hot(hit):
        return jnp.where(owned & hit, 1.0, 0.0).astype(jnp.bfloat16)

    head = dot32(one_hot(rank == within), got_ref[...])
    tail = jnp.zeros((count, lanes), jnp.float32)
    for t in range(3):
        hit = one_hot((within >= CAP) & (rank == within + (4 * t - CAP)))
        tail += dot32(hit, got_ref[:, t * lanes : (t + 1) * lanes])
    a_ref[...] = head[:, : 2 * lanes].astype(jnp.bfloat16)
    b_ref[:, :lanes] = head[:, 2 * lanes : 3 * lanes].astype(jnp.bfloat16)
    b_ref[:, lanes:] = tail.astype(jnp.bfloat16)
    picked = head[:, 3 * lanes :]
    diagonal = lax.broadcasted_iota(jnp.int32, (count, count), 0) == lax.broadcasted_iota(
        jnp.int32, (count, count), 1
    )
    inn_ref[...] = 0.5 * (picked + picked.T) + jnp.where(diagonal, noise_ref[...], 0.0)


def invert_kernel(inn_ref, out_ref):
    size = inn_ref.shape[0]
    step, panels = 8, size // 8
    full = (step, size)
    m = [inn_ref[i * step : (i + 1) * step, :] for i in range(panels)]
    sub = lax.broadcasted_iota(jnp.int32, full, 0)
    lane = lax.broadcasted_iota(jnp.int32, full, 1)
    for p in range(panels):
        at = p * step
        on = lane == sub + at
        row = m[p]
        spread = [jnp.broadcast_to(row[:, at + k : at + k + 1], full) for k in range(step)]
        e = {}
        for i in range(step):
            for k in range(i + 1):
                e[i, k] = jnp.broadcast_to(spread[k][i : i + 1, :], full)
        get = lambda i, k: e[max(i, k), min(i, k)]
        for k in range(step):
            d = 1.0 / e[k, k]
            col = {i: get(i, k) for i in range(step) if i != k}
            scaled = {i: v * d for i, v in col.items()}
            for i in range(step):
                for j in range(i + 1):
                    if i != k and j != k:
                        e[i, j] = e[i, j] - scaled[i] * col[j]
            for i, v in scaled.items():
                e[max(i, k), min(i, k)] = v
            e[k, k] = -d
        less = row - jnp.where(on, 1.0, 0.0)
        rows_b = [jnp.broadcast_to(less[k : k + 1, :], full) for k in range(step)]
        q = []
        for i in range(step):
            terms = [get(i, k) * rows_b[k] for k in range(step)]
            while len(terms) > 1:
                terms = [x + y for x, y in zip(terms[::2], terms[1::2])]
            q.append(terms[0])
        for i in range(panels):
            base = less if i == p else m[i]
            cols = (
                [jnp.broadcast_to(base[:, at + k : at + k + 1], full) for k in range(step)]
            )
            terms = [cols[k] * q[k] for k in range(step)]
            while len(terms) > 1:
                terms = [x + y for x, y in zip(terms[::2], terms[1::2])]
            m[i] = m[i] + terms[0]
            if i == p:
                m[i] = m[i] - jnp.where(on, 2.0, 0.0)
    for i in range(0, panels, 2):
        x = -jnp.concatenate([m[i], m[i + 1]], axis=0)
        for part in range(3):
            piece = x.astype(jnp.bfloat16)
            out_ref[i * step : (i + 2) * step, part * size : (part + 1) * size] = piece
            x = x - piece.astype(jnp.float32)


def update_kernel(width, inverse_ref, cross_ref, slab_ref, *refs):
    pieces, out_ref, held, sem = refs[:8], refs[8], refs[9], refs[10]
    me = lax.axis_index("rows")
    half = width // 2
    inverse, cross = inverse_ref[...], cross_ref[...]
    size = inverse.shape[0]
    y, x, core = 4, 2, 1
    flips = ((0, y), (x, x + y), (0, x), (y, x + y))
    copies = []
    for other in range(2):
        for which in range(4):
            for k in range(2):
                owner = ((me % PLANE) ^ flips[which][k]) ^ (core * other)
                at = owner * width + (which // 2) * half
                at = pl.multiple_of(at, half)
                obs = pieces[other * 4 + which][k]
                gain = sum(
                    dot32(inverse[:, t * size : (t + 1) * size], obs) for t in range(3)
                ).astype(jnp.bfloat16)
                new = slab_ref[:, pl.ds(at, half)].astype(jnp.float32) - dot32(cross, gain)
                index = len(copies)
                held[index] = new.astype(jnp.bfloat16)
                copy = pltpu.make_async_copy(
                    held.at[index], out_ref.at[:, pl.ds(at, half)], sem.at[index]
                )
                copy.start()
                copies.append(copy)
    for copy in copies:
        copy.wait()


def plane_body(slab, cross, obs_index, noise):
    groups = lax.axis_size("rows")
    rows, columns = slab.shape
    count = cross.shape[1]
    width = columns // PLANE
    half = width // 2
    obs = obs_index.reshape(1, count)
    picked = pl.pallas_call(
        functools.partial(pick_kernel, groups, width),
        out_shape=jax.ShapeDtypeStruct((groups * SLOTS, 3 * width // 4 + count), jnp.bfloat16),
        in_specs=[VMEM] * 3,
        out_specs=VMEM,
        name="pick",
    )(obs, slab, cross)
    got = lax.all_to_all(
        picked.reshape(groups, SLOTS, -1), "rows", split_axis=0, concat_axis=0, tiled=True
    ).reshape(groups * SLOTS, -1)
    block = jax.ShapeDtypeStruct((count, half), jnp.bfloat16)
    a0, b0, innovation = pl.pallas_call(
        functools.partial(compact_kernel, rows),
        out_shape=(block, block, jax.ShapeDtypeStruct((count, count), jnp.float32)),
        in_specs=[VMEM] * 3,
        out_specs=(VMEM,) * 3,
        name="compact",
    )(obs, noise.reshape(1, count), got)
    inverse = pl.pallas_call(
        invert_kernel,
        out_shape=jax.ShapeDtypeStruct((count, 3 * count), jnp.bfloat16),
        in_specs=[VMEM],
        out_specs=VMEM,
        cost_estimate=pl.CostEstimate(
            flops=2 * count**3, bytes_accessed=4 * count * count, transcendentals=count
        ),
        name="invert",
    )(innovation)

    def swap(value, bit):
        return lax.ppermute(value, "rows", [(i, i ^ bit) for i in range(groups)])

    y, x, core = 4, 2, 1
    a1, b1 = swap(a0, y), swap(b0, x)
    a01, b01 = jnp.stack([a0, a1]), jnp.stack([b0, b1])
    a23, b23 = swap(a01, x), swap(b01, y)
    own = (a01, a23, b01, b23)
    other = tuple(swap(v, core) for v in own)
    return pl.pallas_call(
        functools.partial(update_kernel, width),
        out_shape=jax.ShapeDtypeStruct(slab.shape, jnp.bfloat16),
        in_specs=[VMEM] * 11,
        out_specs=pl.BlockSpec(memory_space=pl.ANY),
        scratch_shapes=[
            pltpu.VMEM((16, rows, half), jnp.bfloat16),
            pltpu.SemaphoreType.DMA((16,)),
        ],
        name="update",
    )(inverse, cross, slab, *own, *other)


def solution(mesh):
    plane = mesh.shape["cols"] == 1 and mesh.shape["rows"] == 4 * PLANE
    return jax.shard_map(
        plane_body if plane else general_body,
        mesh=mesh,
        in_specs=(P("rows", "cols"), P("rows", "cols"), P(), P()),
        out_specs=P("rows", "cols"),
        check_vma=False,
    )
```

```python
import functools

import jax
import jax.numpy as jnp
from jax import lax
from jax.experimental import pallas as pl
from jax.experimental.pallas import tpu as pltpu
from jax.sharding import PartitionSpec as P

CAP = 12
SLOTS = 16
PLANE = 8
PARTS = 3
VMEM = pl.BlockSpec(memory_space=pltpu.VMEM)
HBM = pl.BlockSpec(memory_space=pltpu.HBM)
MIB = 1 << 20


def room(mib):
    return pltpu.CompilerParams(vmem_limit_bytes=mib * MIB)


def dot32(a, b):
    return jnp.dot(a, b, preferred_element_type=jnp.float32)


def solve_gain(factor, right_side):
    forward = lax.linalg.triangular_solve(factor, right_side, left_side=True, lower=True)
    return lax.linalg.triangular_solve(
        factor, forward, left_side=True, lower=True, transpose_a=True
    )


def make_factor(picked_half, noise):
    picked = lax.all_gather(picked_half, "cols", axis=1, tiled=True).astype(jnp.float32)
    innovation = 0.5 * (picked + picked.T) + jnp.diag(noise)
    return jnp.linalg.cholesky(innovation)


def general_body(slab, cross, obs_index, noise):
    row_count = slab.shape[0]
    groups = lax.axis_size("rows")
    owners = obs_index // row_count
    local_row = obs_index % row_count
    owner_hit = (owners[:, None] == jnp.arange(groups, dtype=jnp.int32)[None, :]).astype(jnp.int32)
    before = jnp.cumsum(owner_hit, axis=0) - owner_hit
    slot_rank = jnp.sum(before * owner_hit, axis=1)
    mine = owners == lax.axis_index("rows")
    slot_hit = (
        mine[:, None] & (slot_rank[:, None] == jnp.arange(CAP, dtype=jnp.int32)[None, :])
    ).astype(jnp.bfloat16)
    row_hit = (local_row[:, None] == jnp.arange(row_count, dtype=jnp.int32)[None, :]).astype(
        jnp.bfloat16
    )
    selector = dot32(slot_hit.T, row_hit).astype(jnp.bfloat16)
    packed_cross = dot32(selector, cross).astype(jnp.bfloat16)
    packed_slab = dot32(selector, slab).astype(jnp.bfloat16)
    placed = owners * CAP + slot_rank
    all_cross, all_slab = (
        lax.all_gather(packed_cross, "rows", axis=0, tiled=True),
        lax.all_gather(packed_slab, "rows", axis=0, tiled=True),
    )
    factor = make_factor(all_cross[placed], noise)
    observed = all_slab[placed].astype(jnp.float32)
    gain = solve_gain(factor, observed).astype(jnp.bfloat16)
    update = dot32(lax.all_gather(cross, "cols", axis=1, tiled=True), gain)
    return (slab.astype(jnp.float32) - update).astype(jnp.bfloat16)


def spread_index(obs_ref, rows):
    count = obs_ref.shape[1]
    along = jnp.broadcast_to(obs_ref[...], (count, count))
    down = along.astype(jnp.float32).T.astype(jnp.int32)
    earlier_row = lax.broadcasted_iota(jnp.int32, (count, count), 0)
    earlier_col = lax.broadcasted_iota(jnp.int32, (count, count), 1)
    same = along // rows == down // rows
    rank_along = jnp.sum(
        jnp.where(same & (earlier_row < earlier_col), 1.0, 0.0), axis=0, keepdims=True
    ).astype(jnp.int32)
    rank_down = jnp.sum(
        jnp.where(same & (earlier_col < earlier_row), 1.0, 0.0), axis=1, keepdims=True
    ).astype(jnp.int32)
    return along, down, rank_along, rank_down


def pick_kernel(groups, width, obs_hbm, slab_hbm, cross_hbm, out_ref, obs_ref, slab, cross, sem):
    rows, count = slab.shape[0], obs_ref.shape[1]

    def fetch(source, target, index):
        copy = pltpu.make_async_copy(source, target, sem.at[index])
        copy.start()
        return copy

    def columns(ref, group):
        return ref.at[:, group * width : (group + 1) * width]

    got_obs = fetch(obs_hbm, obs_ref, PLANE)
    got_slab = [fetch(columns(slab_hbm, g), columns(slab, g), g) for g in range(PLANE)]
    got_cross = fetch(cross_hbm, cross, PLANE + 1)
    me = lax.axis_index("rows")
    got_obs.wait()
    along, down, rank, _ = spread_index(obs_ref, rows)
    picks = 4 * SLOTS
    slot = lax.broadcasted_iota(jnp.int32, (picks, count), 0)
    within, part = slot % SLOTS, slot // SLOTS
    wanted = jnp.where(
        part == 0,
        jnp.where(within < CAP, within, -1),
        jnp.where(within >= CAP, 4 * (part - 1) + within - CAP, -1),
    )
    mine = (along[:1] // rows) == me
    hit = jnp.where(mine & (rank == wanted), 1.0, 0.0).astype(jnp.bfloat16)
    local = lax.broadcasted_iota(jnp.int32, (count, rows), 1) == down[:, :rows] % rows
    selector = dot32(hit, jnp.where(local, 1.0, 0.0).astype(jnp.bfloat16)).astype(jnp.bfloat16)
    got_cross.wait()
    cross_part = dot32(selector[:SLOTS], cross[...]).astype(jnp.bfloat16)
    lanes = width // 4
    for group in range(PLANE):
        got_slab[group].wait()
        got = dot32(selector, slab[:, group * width : (group + 1) * width])
        tail = got[:, 3 * lanes :]
        block = jnp.concatenate(
            [
                (
                    got[:SLOTS, t * lanes : (t + 1) * lanes]
                    + tail[(t + 1) * SLOTS : (t + 2) * SLOTS]
                ).astype(jnp.bfloat16)
                for t in range(3)
            ]
            + [cross_part],
            axis=1,
        )
        for level in range(groups // PLANE):
            at = (level * PLANE + group) * SLOTS
            out_ref[at : at + SLOTS, :] = block


def order_kernel(rows, obs_ref, noise_ref, order_ref, diagonal_ref):
    count, slots = obs_ref.shape[1], order_ref.shape[1]
    _, down, _, rank = spread_index(obs_ref, rows)
    owner = down[:, :1] // rows
    lane = lax.broadcasted_iota(jnp.int32, (count, slots), 1)
    within = lane % SLOTS
    owned = owner == lane // SLOTS
    for t in range(4):
        hit = (
            rank == within
            if t == 0
            else (within >= CAP) & (rank == within + (4 * (t - 1) - CAP))
        )
        order_ref[t * count : (t + 1) * count, :] = jnp.where(owned & hit, 1.0, 0.0).astype(
            jnp.bfloat16
        )
    square = (count, count)
    on = lax.broadcasted_iota(jnp.int32, square, 0) == lax.broadcasted_iota(jnp.int32, square, 1)
    diagonal_ref[...] = jnp.where(on, noise_ref[...], 0.0)


def compact_kernel(order_ref, diagonal_ref, got_ref, observed_ref, inn_ref):
    count = diagonal_ref.shape[0]
    lanes = got_ref.shape[1] // 4
    head = dot32(order_ref[:count, :], got_ref[...])
    tail = jnp.zeros((count, lanes), jnp.float32)
    for t in range(3):
        hit = order_ref[(t + 1) * count : (t + 2) * count, :]
        tail += dot32(hit, got_ref[:, t * lanes : (t + 1) * lanes])
    observed_ref[:, : 3 * lanes] = head[:, : 3 * lanes].astype(jnp.bfloat16)
    observed_ref[:, 3 * lanes :] = tail.astype(jnp.bfloat16)
    picked = head[:, 3 * lanes :]
    inn_ref[...] = 0.5 * (picked + picked.T) + diagonal_ref[...]


def invert_kernel(inn_ref, out_ref):
    size = inn_ref.shape[0]
    step, panels = 8, size // 8
    full = (step, size)
    m = [inn_ref[i * step : (i + 1) * step, :] for i in range(panels)]
    sub = lax.broadcasted_iota(jnp.int32, full, 0)
    lane = lax.broadcasted_iota(jnp.int32, full, 1)
    for p in range(panels):
        at = p * step
        on = lane == sub + at
        row = m[p]
        spread = [jnp.broadcast_to(row[:, at + k : at + k + 1], full) for k in range(step)]
        e = {}
        for i in range(step):
            for k in range(i + 1):
                e[i, k] = jnp.broadcast_to(spread[k][i : i + 1, :], full)
        get = lambda i, k: e[max(i, k), min(i, k)]
        for k in range(step):
            d = 1.0 / e[k, k]
            col = {i: get(i, k) for i in range(step) if i != k}
            scaled = {i: v * d for i, v in col.items()}
            for i in range(step):
                for j in range(i + 1):
                    if i != k and j != k:
                        e[i, j] = e[i, j] - scaled[i] * col[j]
            for i, v in scaled.items():
                e[max(i, k), min(i, k)] = v
            e[k, k] = -d
        less = row - jnp.where(on, 1.0, 0.0)
        rows_b = [jnp.broadcast_to(less[k : k + 1, :], full) for k in range(step)]
        q = []
        for i in range(step):
            terms = [get(i, k) * rows_b[k] for k in range(step)]
            while len(terms) > 1:
                terms = [x + y for x, y in zip(terms[::2], terms[1::2])]
            q.append(terms[0])
        for i in range(panels):
            base = less if i == p else m[i]
            cols = (
                [jnp.broadcast_to(base[:, at + k : at + k + 1], full) for k in range(step)]
            )
            terms = [cols[k] * q[k] for k in range(step)]
            while len(terms) > 1:
                terms = [x + y for x, y in zip(terms[::2], terms[1::2])]
            m[i] = m[i] + terms[0]
            if i == p:
                m[i] = m[i] - jnp.where(on, 2.0, 0.0)
    for i in range(0, panels, 2):
        x = -jnp.concatenate([m[i], m[i + 1]], axis=0)
        for part in range(PARTS):
            piece = x.astype(jnp.bfloat16)
            at = part * size + i * step
            out_ref[at : at + 2 * step, :] = piece
            x = x - piece.astype(jnp.float32)


def update_kernel(width, flips, inverse_ref, cross_ref, slab_ref, *refs):
    pieces, (out_ref, held, sem) = refs[: len(flips)], refs[-3:]
    place = lax.axis_index("rows") % PLANE
    inverse, cross = inverse_ref[...], cross_ref[...]
    size = cross.shape[1]
    copies = []
    for index, flip in enumerate(flips):
        at = pl.multiple_of((place ^ flip) * width, width)
        parts = dot32(inverse, pieces[index][...])
        gain = sum(parts[t * size : (t + 1) * size] for t in range(PARTS)).astype(jnp.bfloat16)
        new = slab_ref[:, pl.ds(at, width)].astype(jnp.float32) - dot32(cross, gain)
        held[index] = new.astype(jnp.bfloat16)
        copies.append(
            pltpu.make_async_copy(held.at[index], out_ref.at[:, pl.ds(at, width)], sem.at[index])
        )
    for copy in copies:
        copy.start()
    for copy in copies:
        copy.wait()


def plane_body(slab, cross, obs_index, noise):
    groups = lax.axis_size("rows")
    rows, columns = slab.shape
    count = cross.shape[1]
    width = columns // PLANE
    obs = obs_index.reshape(1, count)
    picked = pl.pallas_call(
        functools.partial(pick_kernel, groups, width),
        out_shape=jax.ShapeDtypeStruct((groups * SLOTS, 3 * width // 4 + count), jnp.bfloat16),
        in_specs=[HBM] * 3,
        out_specs=VMEM,
        scratch_shapes=[
            pltpu.VMEM((1, count), jnp.int32),
            pltpu.VMEM(slab.shape, jnp.bfloat16),
            pltpu.VMEM(cross.shape, jnp.bfloat16),
            pltpu.SemaphoreType.DMA((PLANE + 2,)),
        ],
        compiler_params=room(56),
        name="pick",
    )(obs, slab, cross)
    order, diagonal = pl.pallas_call(
        functools.partial(order_kernel, rows),
        out_shape=(
            jax.ShapeDtypeStruct((4 * count, groups * SLOTS), jnp.bfloat16),
            jax.ShapeDtypeStruct((count, count), jnp.float32),
        ),
        in_specs=[VMEM] * 2,
        out_specs=(VMEM,) * 2,
        cost_estimate=pl.CostEstimate(
            flops=1000 * count**3, bytes_accessed=4 * count * count, transcendentals=0
        ),
        compiler_params=room(8),
        name="order",
    )(obs, noise.reshape(1, count))
    got = lax.all_to_all(
        picked.reshape(groups, SLOTS, -1), "rows", split_axis=0, concat_axis=0, tiled=True
    ).reshape(groups * SLOTS, -1)
    observed, innovation = pl.pallas_call(
        compact_kernel,
        out_shape=(
            jax.ShapeDtypeStruct((count, width), jnp.bfloat16),
            jax.ShapeDtypeStruct((count, count), jnp.float32),
        ),
        in_specs=[VMEM] * 3,
        out_specs=(VMEM,) * 2,
        compiler_params=room(8),
        name="compact",
    )(order, diagonal, got)
    inverse = pl.pallas_call(
        invert_kernel,
        out_shape=jax.ShapeDtypeStruct((PARTS * count, count), jnp.bfloat16),
        in_specs=[VMEM],
        out_specs=VMEM,
        cost_estimate=pl.CostEstimate(
            flops=3000 * count**3, bytes_accessed=4 * count * count, transcendentals=count
        ),
        compiler_params=room(4),
        name="invert",
    )(innovation)

    def swap(value, bit):
        return lax.ppermute(value, "rows", [(i, i ^ bit) for i in range(groups)])

    def update(inverse, flips, pieces, before):
        more = () if before is None else (before,)
        return pl.pallas_call(
            functools.partial(update_kernel, width, flips),
            out_shape=jax.ShapeDtypeStruct(slab.shape, jnp.bfloat16),
            in_specs=[VMEM] * (3 + len(pieces)) + [HBM] * len(more),
            out_specs=HBM,
            scratch_shapes=[
                pltpu.VMEM((len(flips), rows, width), jnp.bfloat16),
                pltpu.SemaphoreType.DMA((len(flips),)),
            ],
            input_output_aliases={3 + len(pieces): 0} if more else {},
            compiler_params=room(8),
            name="update",
        )(inverse, cross, slab, *pieces, *more)

    y, x, core = 4, 2, 1
    by = {0: observed}
    for flip in (x + y, x, y, core):
        by[flip] = swap(observed, flip)
    arrived, inverse = lax.optimization_barrier(([by[f] for f in (x, y, x + y)], inverse))
    for flip, piece in zip((x, y, x + y), arrived):
        by[flip] = piece
        by[flip + core] = swap(piece, core)
    early, late = (0, core, x, y, x + y), (x + core, y + core, x + y + core)
    half = update(inverse, early, [by[f] for f in early], None)
    return update(inverse, late, [by[f] for f in late], half)


def solution(mesh):
    plane = mesh.shape["cols"] == 1 and mesh.shape["rows"] == 4 * PLANE
    return jax.shard_map(
        plane_body if plane else general_body,
        mesh=mesh,
        in_specs=(P("rows", "cols"), P("rows", "cols"), P(), P()),
        out_specs=P("rows", "cols"),
        check_vma=False,
    )
```

```python
import functools

import jax
import jax.numpy as jnp
from jax import lax
from jax.experimental import pallas as pl
from jax.experimental.pallas import tpu as pltpu
from jax.sharding import PartitionSpec as P

CAP = 12
SLOTS = 16
PLANE = 8
PARTS = 3
VMEM = pl.BlockSpec(memory_space=pltpu.VMEM)
HBM = pl.BlockSpec(memory_space=pltpu.HBM)
MIB = 1 << 20


def room(mib):
    return pltpu.CompilerParams(vmem_limit_bytes=mib * MIB)


def dot32(a, b):
    return jnp.dot(a, b, preferred_element_type=jnp.float32)


def solve_gain(factor, right_side):
    forward = lax.linalg.triangular_solve(factor, right_side, left_side=True, lower=True)
    return lax.linalg.triangular_solve(
        factor, forward, left_side=True, lower=True, transpose_a=True
    )


def make_factor(picked_half, noise):
    picked = lax.all_gather(picked_half, "cols", axis=1, tiled=True).astype(jnp.float32)
    innovation = 0.5 * (picked + picked.T) + jnp.diag(noise)
    return jnp.linalg.cholesky(innovation)


def general_body(slab, cross, obs_index, noise):
    row_count = slab.shape[0]
    groups = lax.axis_size("rows")
    owners = obs_index // row_count
    local_row = obs_index % row_count
    owner_hit = (owners[:, None] == jnp.arange(groups, dtype=jnp.int32)[None, :]).astype(jnp.int32)
    before = jnp.cumsum(owner_hit, axis=0) - owner_hit
    slot_rank = jnp.sum(before * owner_hit, axis=1)
    mine = owners == lax.axis_index("rows")
    slot_hit = (
        mine[:, None] & (slot_rank[:, None] == jnp.arange(CAP, dtype=jnp.int32)[None, :])
    ).astype(jnp.bfloat16)
    row_hit = (local_row[:, None] == jnp.arange(row_count, dtype=jnp.int32)[None, :]).astype(
        jnp.bfloat16
    )
    selector = dot32(slot_hit.T, row_hit).astype(jnp.bfloat16)
    packed_cross = dot32(selector, cross).astype(jnp.bfloat16)
    packed_slab = dot32(selector, slab).astype(jnp.bfloat16)
    placed = owners * CAP + slot_rank
    all_cross, all_slab = (
        lax.all_gather(packed_cross, "rows", axis=0, tiled=True),
        lax.all_gather(packed_slab, "rows", axis=0, tiled=True),
    )
    factor = make_factor(all_cross[placed], noise)
    observed = all_slab[placed].astype(jnp.float32)
    gain = solve_gain(factor, observed).astype(jnp.bfloat16)
    update = dot32(lax.all_gather(cross, "cols", axis=1, tiled=True), gain)
    return (slab.astype(jnp.float32) - update).astype(jnp.bfloat16)


def spread_index(obs_ref, rows):
    count = obs_ref.shape[1]
    along = jnp.broadcast_to(obs_ref[...], (count, count))
    down = along.astype(jnp.float32).T.astype(jnp.int32)
    earlier_row = lax.broadcasted_iota(jnp.int32, (count, count), 0)
    earlier_col = lax.broadcasted_iota(jnp.int32, (count, count), 1)
    same = along // rows == down // rows
    rank_along = jnp.sum(
        jnp.where(same & (earlier_row < earlier_col), 1.0, 0.0), axis=0, keepdims=True
    ).astype(jnp.int32)
    rank_down = jnp.sum(
        jnp.where(same & (earlier_col < earlier_row), 1.0, 0.0), axis=1, keepdims=True
    ).astype(jnp.int32)
    return along, down, rank_along, rank_down


def column_group(device):
    return (device % PLANE) ^ (6 * ((device // PLANE) % 2))


def pick_kernel(
    groups, width, obs_hbm, slab_hbm, cross_hbm, out_hbm, obs_ref, slab, cross, out, sem, out_sem
):
    rows, count = slab.shape[0], obs_ref.shape[1]
    half = slab.shape[1] // 2

    def fetch(source, target, index):
        copy = pltpu.make_async_copy(source, target, sem.at[index])
        copy.start()
        return copy

    got_obs = fetch(obs_hbm, obs_ref, 0)
    got_cross = fetch(cross_hbm, cross, 1)
    got_slab = [
        fetch(slab_hbm.at[:, i * half : (i + 1) * half], slab.at[:, i * half : (i + 1) * half], 2 + i)
        for i in range(2)
    ]
    me = lax.axis_index("rows")
    got_obs.wait()
    along, down, rank, _ = spread_index(obs_ref, rows)
    picks = 4 * SLOTS
    slot = lax.broadcasted_iota(jnp.int32, (picks, count), 0)
    within, part = slot % SLOTS, slot // SLOTS
    wanted = jnp.where(
        part == 0,
        jnp.where(within < CAP, within, -1),
        jnp.where(within >= CAP, 4 * (part - 1) + within - CAP, -1),
    )
    mine = (along[:1] // rows) == me
    hit = jnp.where(mine & (rank == wanted), 1.0, 0.0).astype(jnp.bfloat16)
    local = lax.broadcasted_iota(jnp.int32, (count, rows), 1) == down[:, :rows] % rows
    selector = dot32(hit, jnp.where(local, 1.0, 0.0).astype(jnp.bfloat16)).astype(jnp.bfloat16)
    got_cross.wait()
    cross_part = dot32(selector[:SLOTS], cross[...]).astype(jnp.bfloat16)
    lanes = width // 4
    sent = []
    for group in range(PLANE):
        if group % 4 == 0:
            got_slab[group // 4].wait()
        got = dot32(selector, slab[:, group * width : (group + 1) * width])
        tail = got[:, 3 * lanes :]
        out[group * SLOTS : (group + 1) * SLOTS, :] = jnp.concatenate(
            [
                (
                    got[:SLOTS, t * lanes : (t + 1) * lanes]
                    + tail[(t + 1) * SLOTS : (t + 2) * SLOTS]
                ).astype(jnp.bfloat16)
                for t in range(3)
            ]
            + [cross_part],
            axis=1,
        )
        if group % 2:
            source = out.at[(group - 1) * SLOTS : (group + 1) * SLOTS]
            for level in range(groups // PLANE):
                to = (level * PLANE + column_group(level * PLANE + group - 1)) * SLOTS
                copy = pltpu.make_async_copy(
                    source, out_hbm.at[to : to + 2 * SLOTS], out_sem.at[len(sent)]
                )
                copy.start()
                sent.append(copy)
    for copy in sent:
        copy.wait()


def order_kernel(rows, obs_ref, noise_ref, order_ref, diagonal_ref):
    count, slots = obs_ref.shape[1], order_ref.shape[1]
    _, down, _, rank = spread_index(obs_ref, rows)
    owner = down[:, :1] // rows
    lane = lax.broadcasted_iota(jnp.int32, (count, slots), 1)
    within = lane % SLOTS
    owned = owner == lane // SLOTS
    for t in range(4):
        hit = (
            rank == within
            if t == 0
            else (within >= CAP) & (rank == within + (4 * (t - 1) - CAP))
        )
        order_ref[t * count : (t + 1) * count, :] = jnp.where(owned & hit, 1.0, 0.0).astype(
            jnp.bfloat16
        )
    square = (count, count)
    on = lax.broadcasted_iota(jnp.int32, square, 0) == lax.broadcasted_iota(jnp.int32, square, 1)
    diagonal_ref[...] = jnp.where(on, noise_ref[...], 0.0)


def compact_kernel(order_ref, diagonal_ref, got_ref, observed_ref, inn_ref):
    count = diagonal_ref.shape[0]
    lanes = got_ref.shape[1] // 4
    head = dot32(order_ref[:count, :], got_ref[...])
    tail = jnp.zeros((count, lanes), jnp.float32)
    for t in range(3):
        hit = order_ref[(t + 1) * count : (t + 2) * count, :]
        tail += dot32(hit, got_ref[:, t * lanes : (t + 1) * lanes])
    observed_ref[:, : 3 * lanes] = head[:, : 3 * lanes].astype(jnp.bfloat16)
    observed_ref[:, 3 * lanes :] = tail.astype(jnp.bfloat16)
    picked = head[:, 3 * lanes :]
    inn_ref[...] = 0.5 * (picked + picked.T) + diagonal_ref[...]


def invert_kernel(panel_range, inn_ref, out_ref):
    size = inn_ref.shape[0]
    step, panels = 8, size // 8
    full = (step, size)
    m = [inn_ref[i * step : (i + 1) * step, :] for i in range(panels)]
    sub = lax.broadcasted_iota(jnp.int32, full, 0)
    lane = lax.broadcasted_iota(jnp.int32, full, 1)
    for p in panel_range:
        at = p * step
        on = lane == sub + at
        row = m[p]
        spread = [jnp.broadcast_to(row[:, at + k : at + k + 1], full) for k in range(step)]
        e = {}
        for i in range(step):
            for k in range(i + 1):
                e[i, k] = jnp.broadcast_to(spread[k][i : i + 1, :], full)
        get = lambda i, k: e[max(i, k), min(i, k)]
        for k in range(step):
            d = 1.0 / e[k, k]
            col = {i: get(i, k) for i in range(step) if i != k}
            scaled = {i: v * d for i, v in col.items()}
            for i in range(step):
                for j in range(i + 1):
                    if i != k and j != k:
                        e[i, j] = e[i, j] - scaled[i] * col[j]
            for i, v in scaled.items():
                e[max(i, k), min(i, k)] = v
            e[k, k] = -d
        less = row - jnp.where(on, 1.0, 0.0)
        rows_b = [jnp.broadcast_to(less[k : k + 1, :], full) for k in range(step)]
        q = []
        for i in range(step):
            terms = [get(i, k) * rows_b[k] for k in range(step)]
            while len(terms) > 1:
                terms = [x + y for x, y in zip(terms[::2], terms[1::2])]
            q.append(terms[0])
        for i in range(panels):
            base = less if i == p else m[i]
            cols = (
                [jnp.broadcast_to(base[:, at + k : at + k + 1], full) for k in range(step)]
            )
            terms = [cols[k] * q[k] for k in range(step)]
            while len(terms) > 1:
                terms = [x + y for x, y in zip(terms[::2], terms[1::2])]
            m[i] = m[i] + terms[0]
            if i == p:
                m[i] = m[i] - jnp.where(on, 2.0, 0.0)
    if panel_range[-1] < panels - 1:
        for i in range(panels):
            out_ref[i * step : (i + 1) * step, :] = m[i]
        return
    for i in range(0, panels, 2):
        x = -jnp.concatenate([m[i], m[i + 1]], axis=0)
        for part in range(PARTS):
            piece = x.astype(jnp.bfloat16)
            at = part * size + i * step
            out_ref[at : at + 2 * step, :] = piece
            x = x - piece.astype(jnp.float32)


def update_kernel(width, flips, inverse_ref, cross_ref, slab_ref, *refs):
    pieces, (out_ref, held, sem) = refs[: len(flips)], refs[-3:]
    place = column_group(lax.axis_index("rows"))
    cross = cross_ref[...]
    size = cross.shape[1]
    inverse = jnp.concatenate(
        [inverse_ref[t * size : (t + 1) * size] for t in range(PARTS)], axis=1
    )
    copies, gains = [], []
    for piece in pieces:
        gains.append(
            dot32(inverse, jnp.concatenate([piece[...]] * PARTS, axis=0)).astype(jnp.bfloat16)
        )
    for index, flip in enumerate(flips):
        at = pl.multiple_of((place ^ flip) * width, width)
        new = slab_ref[:, pl.ds(at, width)].astype(jnp.float32) - dot32(cross, gains[index])
        held[index] = new.astype(jnp.bfloat16)
        copy = pltpu.make_async_copy(
            held.at[index], out_ref.at[:, pl.ds(at, width)], sem.at[index]
        )
        copy.start()
        copies.append(copy)
    for copy in copies:
        copy.wait()


def plane_body(slab, cross, obs_index, noise):
    groups = lax.axis_size("rows")
    rows, columns = slab.shape
    count = cross.shape[1]
    width = columns // PLANE
    obs = obs_index.reshape(1, count)
    picked = pl.pallas_call(
        functools.partial(pick_kernel, groups, width),
        out_shape=jax.ShapeDtypeStruct((groups * SLOTS, 3 * width // 4 + count), jnp.bfloat16),
        in_specs=[HBM] * 3,
        out_specs=HBM,
        scratch_shapes=[
            pltpu.VMEM((1, count), jnp.int32),
            pltpu.VMEM(slab.shape, jnp.bfloat16),
            pltpu.VMEM(cross.shape, jnp.bfloat16),
            pltpu.VMEM((PLANE * SLOTS, 3 * width // 4 + count), jnp.bfloat16),
            pltpu.SemaphoreType.DMA((4,)),
            pltpu.SemaphoreType.DMA((groups // 2,)),
        ],
        compiler_params=room(56),
        name="pick",
    )(obs, slab, cross)
    order, diagonal = pl.pallas_call(
        functools.partial(order_kernel, rows),
        out_shape=(
            jax.ShapeDtypeStruct((4 * count, groups * SLOTS), jnp.bfloat16),
            jax.ShapeDtypeStruct((count, count), jnp.float32),
        ),
        in_specs=[VMEM] * 2,
        out_specs=(VMEM,) * 2,
        cost_estimate=pl.CostEstimate(
            flops=1000 * count**3, bytes_accessed=4 * count * count, transcendentals=0
        ),
        compiler_params=room(8),
        name="order",
    )(obs, noise.reshape(1, count))
    got = lax.all_to_all(
        picked.reshape(groups, SLOTS, -1), "rows", split_axis=0, concat_axis=0, tiled=True
    ).reshape(groups * SLOTS, -1)
    observed, innovation = pl.pallas_call(
        compact_kernel,
        out_shape=(
            jax.ShapeDtypeStruct((count, width), jnp.bfloat16),
            jax.ShapeDtypeStruct((count, count), jnp.float32),
        ),
        in_specs=[VMEM] * 3,
        out_specs=(VMEM,) * 2,
        compiler_params=room(8),
        name="compact",
    )(order, diagonal, got)
    def invert(panel_range, value, out_shape):
        return pl.pallas_call(
            functools.partial(invert_kernel, panel_range),
            out_shape=out_shape,
            in_specs=[VMEM],
            out_specs=VMEM,
            cost_estimate=pl.CostEstimate(
                flops=1500 * count**3, bytes_accessed=4 * count * count, transcendentals=count
            ),
            compiler_params=room(4),
            name="invert",
        )(value)

    def swap(value, bit):
        return lax.ppermute(value, "rows", [(i, i ^ bit) for i in range(groups)])

    def update(inverse, flips, pieces, before):
        more = () if before is None else (before,)
        return pl.pallas_call(
            functools.partial(update_kernel, width, flips),
            out_shape=jax.ShapeDtypeStruct(slab.shape, jnp.bfloat16),
            in_specs=[VMEM] * (3 + len(pieces)) + [HBM] * len(more),
            out_specs=HBM,
            scratch_shapes=[
                pltpu.VMEM((len(flips), rows, width), jnp.bfloat16),
                pltpu.SemaphoreType.DMA((len(flips),)),
            ],
            input_output_aliases={3 + len(pieces): 0} if more else {},
            compiler_params=room(12),
            name="update",
        )(inverse, cross, slab, *pieces, *more)

    panels = count // 8
    by = {0: observed, 1: swap(observed, 1)}
    by.update({group: swap(observed, bit) for bit, group in ((2, 2), (4, 4), (8, 6))})
    midway = invert(range(panels // 2), innovation, innovation)
    arrived, midway = lax.optimization_barrier(([by[g] for g in (2, 4, 6)], midway))
    for group, piece in zip((2, 4, 6), arrived):
        by[group] = piece
        by[group + 1] = swap(piece, 1)
    inverse = invert(
        range(panels // 2, panels),
        midway,
        jax.ShapeDtypeStruct((PARTS * count, count), jnp.bfloat16),
    )
    flips = tuple(range(PLANE))
    return update(inverse, flips, [by[f] for f in flips], None)


def solution(mesh):
    plane = mesh.shape["cols"] == 1 and mesh.shape["rows"] == 4 * PLANE
    return jax.shard_map(
        plane_body if plane else general_body,
        mesh=mesh,
        in_specs=(P("rows", "cols"), P("rows", "cols"), P(), P()),
        out_specs=P("rows", "cols"),
        check_vma=False,
    )
```

```python
import functools

import jax
import jax.numpy as jnp
from jax import lax
from jax.experimental import pallas as pl
from jax.experimental.pallas import tpu as pltpu
from jax.sharding import PartitionSpec as P

CAP = 12
SLOTS = 16
PLANE = 8
PARTS = 3
VMEM = pl.BlockSpec(memory_space=pltpu.VMEM)
HBM = pl.BlockSpec(memory_space=pltpu.HBM)
MIB = 1 << 20


def room(mib):
    return pltpu.CompilerParams(vmem_limit_bytes=mib * MIB)


def dot32(a, b):
    return jnp.dot(a, b, preferred_element_type=jnp.float32)


def solve_gain(factor, right_side):
    forward = lax.linalg.triangular_solve(factor, right_side, left_side=True, lower=True)
    return lax.linalg.triangular_solve(
        factor, forward, left_side=True, lower=True, transpose_a=True
    )


def make_factor(picked_half, noise):
    picked = lax.all_gather(picked_half, "cols", axis=1, tiled=True).astype(jnp.float32)
    innovation = 0.5 * (picked + picked.T) + jnp.diag(noise)
    return jnp.linalg.cholesky(innovation)


def general_body(slab, cross, obs_index, noise):
    row_count = slab.shape[0]
    groups = lax.axis_size("rows")
    owners = obs_index // row_count
    local_row = obs_index % row_count
    owner_hit = (owners[:, None] == jnp.arange(groups, dtype=jnp.int32)[None, :]).astype(jnp.int32)
    before = jnp.cumsum(owner_hit, axis=0) - owner_hit
    slot_rank = jnp.sum(before * owner_hit, axis=1)
    mine = owners == lax.axis_index("rows")
    slot_hit = (
        mine[:, None] & (slot_rank[:, None] == jnp.arange(CAP, dtype=jnp.int32)[None, :])
    ).astype(jnp.bfloat16)
    row_hit = (local_row[:, None] == jnp.arange(row_count, dtype=jnp.int32)[None, :]).astype(
        jnp.bfloat16
    )
    selector = dot32(slot_hit.T, row_hit).astype(jnp.bfloat16)
    packed_cross = dot32(selector, cross).astype(jnp.bfloat16)
    packed_slab = dot32(selector, slab).astype(jnp.bfloat16)
    placed = owners * CAP + slot_rank
    all_cross, all_slab = (
        lax.all_gather(packed_cross, "rows", axis=0, tiled=True),
        lax.all_gather(packed_slab, "rows", axis=0, tiled=True),
    )
    factor = make_factor(all_cross[placed], noise)
    observed = all_slab[placed].astype(jnp.float32)
    gain = solve_gain(factor, observed).astype(jnp.bfloat16)
    update = dot32(lax.all_gather(cross, "cols", axis=1, tiled=True), gain)
    return (slab.astype(jnp.float32) - update).astype(jnp.bfloat16)


def spread_index(obs_ref, rows):
    count = obs_ref.shape[1]
    along = jnp.broadcast_to(obs_ref[...], (count, count))
    down = along.astype(jnp.float32).T.astype(jnp.int32)
    earlier_row = lax.broadcasted_iota(jnp.int32, (count, count), 0)
    earlier_col = lax.broadcasted_iota(jnp.int32, (count, count), 1)
    same = along // rows == down // rows
    rank_along = jnp.sum(
        jnp.where(same & (earlier_row < earlier_col), 1.0, 0.0), axis=0, keepdims=True
    ).astype(jnp.int32)
    rank_down = jnp.sum(
        jnp.where(same & (earlier_col < earlier_row), 1.0, 0.0), axis=1, keepdims=True
    ).astype(jnp.int32)
    return along, down, rank_along, rank_down


def column_group(device):
    return (device % PLANE) ^ (6 * ((device // PLANE) % 2))


def pick_kernel(
    groups, width, obs_hbm, slab_hbm, cross_hbm, out_hbm, picked_hbm, obs_ref, slab, cross, out, picked, sem, out_sem
):
    rows, count = slab.shape[0], obs_ref.shape[1]
    half = slab.shape[1] // 2

    def fetch(source, target, index):
        copy = pltpu.make_async_copy(source, target, sem.at[index])
        copy.start()
        return copy

    got_obs = fetch(obs_hbm, obs_ref, 0)
    got_cross = fetch(cross_hbm, cross, 1)
    got_slab = [
        fetch(slab_hbm.at[:, i * half : (i + 1) * half], slab.at[:, i * half : (i + 1) * half], 2 + i)
        for i in range(2)
    ]
    me = lax.axis_index("rows")
    got_obs.wait()
    along, down, rank, _ = spread_index(obs_ref, rows)
    picks = 4 * SLOTS
    slot = lax.broadcasted_iota(jnp.int32, (picks, count), 0)
    within, part = slot % SLOTS, slot // SLOTS
    wanted = jnp.where(
        part == 0,
        jnp.where(within < CAP, within, -1),
        jnp.where(within >= CAP, 4 * (part - 1) + within - CAP, -1),
    )
    mine = (along[:1] // rows) == me
    hit = jnp.where(mine & (rank == wanted), 1.0, 0.0).astype(jnp.bfloat16)
    local = lax.broadcasted_iota(jnp.int32, (count, rows), 1) == down[:, :rows] % rows
    selector = dot32(hit, jnp.where(local, 1.0, 0.0).astype(jnp.bfloat16)).astype(jnp.bfloat16)
    got_cross.wait()
    picked[...] = dot32(selector[:SLOTS], cross[...]).astype(jnp.bfloat16)
    lanes = width // 4
    sent = [pltpu.make_async_copy(picked, picked_hbm, out_sem.at[0])]
    sent[0].start()
    for group in range(PLANE):
        if group % 4 == 0:
            got_slab[group // 4].wait()
        got = dot32(selector, slab[:, group * width : (group + 1) * width])
        tail = got[:, 3 * lanes :]
        out[group * SLOTS : (group + 1) * SLOTS, :] = jnp.concatenate(
            [
                (
                    got[:SLOTS, t * lanes : (t + 1) * lanes]
                    + tail[(t + 1) * SLOTS : (t + 2) * SLOTS]
                ).astype(jnp.bfloat16)
                for t in range(3)
            ],
            axis=1,
        )
        if group % 2:
            source = out.at[(group - 1) * SLOTS : (group + 1) * SLOTS]
            for level in range(groups // PLANE):
                to = (level * PLANE + column_group(level * PLANE + group - 1)) * SLOTS
                copy = pltpu.make_async_copy(
                    source, out_hbm.at[to : to + 2 * SLOTS], out_sem.at[len(sent)]
                )
                copy.start()
                sent.append(copy)
    for copy in sent:
        copy.wait()


def order_kernel(rows, obs_ref, noise_ref, order_ref, cross_order_ref, diagonal_ref):
    count, slots = obs_ref.shape[1], order_ref.shape[1]
    _, down, _, rank = spread_index(obs_ref, rows)
    owner = down[:, :1] // rows
    lane = lax.broadcasted_iota(jnp.int32, (count, slots), 1)
    within, device = lane % SLOTS, lane // SLOTS

    def one_hot(hit):
        return jnp.where(hit, 1.0, 0.0).astype(jnp.bfloat16)

    owned = owner == device
    order_ref[:count, :] = one_hot(owned & (rank == within))
    for t in range(3):
        hit = (within >= CAP) & (rank == within + (4 * t - CAP))
        order_ref[(t + 1) * count : (t + 2) * count, :] = one_hot(owned & hit)
    apart = owner ^ lax.axis_index("rows")
    cross_order_ref[...] = one_hot((apart == device) & (rank == within))
    square = (count, count)
    on = lax.broadcasted_iota(jnp.int32, square, 0) == lax.broadcasted_iota(jnp.int32, square, 1)
    diagonal_ref[...] = jnp.where(on, noise_ref[...], 0.0)


def compact_kernel(order_ref, got_ref, observed_ref):
    count = observed_ref.shape[0]
    lanes = got_ref.shape[1] // 3
    head = dot32(order_ref[:count, :], got_ref[...])
    tail = jnp.zeros((count, lanes), jnp.float32)
    for t in range(3):
        hit = order_ref[(t + 1) * count : (t + 2) * count, :]
        tail += dot32(hit, got_ref[:, t * lanes : (t + 1) * lanes])
    observed_ref[:, : 3 * lanes] = head.astype(jnp.bfloat16)
    observed_ref[:, 3 * lanes :] = tail.astype(jnp.bfloat16)


def innovation_of(order_ref, diagonal_ref, *pieces):
    span = pieces[0].shape[0]
    picked = sum(
        dot32(order_ref[:, i * span : (i + 1) * span], piece[...])
        for i, piece in enumerate(pieces)
    )
    return 0.5 * (picked + picked.T) + diagonal_ref[...]


def invert_kernel(panel_range, *refs):
    sources, out_ref = refs[:-2], refs[-2]
    inn_ref = refs[-1]
    size = inn_ref.shape[0]
    inn_ref[...] = innovation_of(*sources) if len(sources) > 1 else sources[0][...]
    step, panels = 8, size // 8
    full = (step, size)
    m = [inn_ref[i * step : (i + 1) * step, :] for i in range(panels)]
    sub = lax.broadcasted_iota(jnp.int32, full, 0)
    lane = lax.broadcasted_iota(jnp.int32, full, 1)
    for p in panel_range:
        at = p * step
        on = lane == sub + at
        row = m[p]
        spread = [jnp.broadcast_to(row[:, at + k : at + k + 1], full) for k in range(step)]
        e = {}
        for i in range(step):
            for k in range(i + 1):
                e[i, k] = jnp.broadcast_to(spread[k][i : i + 1, :], full)
        get = lambda i, k: e[max(i, k), min(i, k)]
        for k in range(step):
            d = 1.0 / e[k, k]
            col = {i: get(i, k) for i in range(step) if i != k}
            scaled = {i: v * d for i, v in col.items()}
            for i in range(step):
                for j in range(i + 1):
                    if i != k and j != k:
                        e[i, j] = e[i, j] - scaled[i] * col[j]
            for i, v in scaled.items():
                e[max(i, k), min(i, k)] = v
            e[k, k] = -d
        less = row - jnp.where(on, 1.0, 0.0)
        rows_b = [jnp.broadcast_to(less[k : k + 1, :], full) for k in range(step)]
        q = []
        for i in range(step):
            terms = [get(i, k) * rows_b[k] for k in range(step)]
            while len(terms) > 1:
                terms = [x + y for x, y in zip(terms[::2], terms[1::2])]
            q.append(terms[0])
        for i in range(panels):
            base = less if i == p else m[i]
            cols = (
                [jnp.broadcast_to(base[:, at + k : at + k + 1], full) for k in range(step)]
            )
            terms = [cols[k] * q[k] for k in range(step)]
            while len(terms) > 1:
                terms = [x + y for x, y in zip(terms[::2], terms[1::2])]
            m[i] = m[i] + terms[0]
            if i == p:
                m[i] = m[i] - jnp.where(on, 2.0, 0.0)
    if panel_range[-1] < panels - 1:
        for i in range(panels):
            out_ref[i * step : (i + 1) * step, :] = m[i]
        return
    for i in range(0, panels, 2):
        x = -jnp.concatenate([m[i], m[i + 1]], axis=0)
        for part in range(PARTS):
            piece = x.astype(jnp.bfloat16)
            at = part * size + i * step
            out_ref[at : at + 2 * step, :] = piece
            x = x - piece.astype(jnp.float32)


def update_kernel(width, flips, inverse_ref, cross_ref, slab_ref, *refs):
    pieces, (out_ref, held, sem) = refs[: len(flips)], refs[-3:]
    place = column_group(lax.axis_index("rows"))
    cross = cross_ref[...]
    size = cross.shape[1]
    inverse = jnp.concatenate(
        [inverse_ref[t * size : (t + 1) * size] for t in range(PARTS)], axis=1
    )
    copies, gains = [], []
    for piece in pieces:
        gains.append(
            dot32(inverse, jnp.concatenate([piece[...]] * PARTS, axis=0)).astype(jnp.bfloat16)
        )
    for index, flip in enumerate(flips):
        at = pl.multiple_of((place ^ flip) * width, width)
        new = slab_ref[:, pl.ds(at, width)].astype(jnp.float32) - dot32(cross, gains[index])
        held[index] = new.astype(jnp.bfloat16)
        copy = pltpu.make_async_copy(
            held.at[index], out_ref.at[:, pl.ds(at, width)], sem.at[index]
        )
        copy.start()
        copies.append(copy)
    for copy in copies:
        copy.wait()


def plane_body(slab, cross, obs_index, noise):
    groups = lax.axis_size("rows")
    rows, columns = slab.shape
    count = cross.shape[1]
    width = columns // PLANE
    obs = obs_index.reshape(1, count)
    packed, picked = pl.pallas_call(
        functools.partial(pick_kernel, groups, width),
        out_shape=(
            jax.ShapeDtypeStruct((groups * SLOTS, 3 * width // 4), jnp.bfloat16),
            jax.ShapeDtypeStruct((SLOTS, count), jnp.bfloat16),
        ),
        in_specs=[HBM] * 3,
        out_specs=(HBM, HBM),
        scratch_shapes=[
            pltpu.VMEM((1, count), jnp.int32),
            pltpu.VMEM(slab.shape, jnp.bfloat16),
            pltpu.VMEM(cross.shape, jnp.bfloat16),
            pltpu.VMEM((PLANE * SLOTS, 3 * width // 4), jnp.bfloat16),
            pltpu.VMEM((SLOTS, count), jnp.bfloat16),
            pltpu.SemaphoreType.DMA((4,)),
            pltpu.SemaphoreType.DMA((1 + groups // 2,)),
        ],
        compiler_params=room(56),
        name="pick",
    )(obs, slab, cross)
    order, cross_order, diagonal = pl.pallas_call(
        functools.partial(order_kernel, rows),
        out_shape=(
            jax.ShapeDtypeStruct((4 * count, groups * SLOTS), jnp.bfloat16),
            jax.ShapeDtypeStruct((count, groups * SLOTS), jnp.bfloat16),
            jax.ShapeDtypeStruct((count, count), jnp.float32),
        ),
        in_specs=[VMEM] * 2,
        out_specs=(VMEM,) * 3,
        cost_estimate=pl.CostEstimate(
            flops=1000 * count**3, bytes_accessed=4 * count * count, transcendentals=0
        ),
        compiler_params=room(8),
        name="order",
    )(obs, noise.reshape(1, count))

    def swap(value, bit):
        return lax.ppermute(value, "rows", [(i, i ^ bit) for i in range(groups)])

    got = lax.all_to_all(
        packed.reshape(groups, SLOTS, -1), "rows", split_axis=0, concat_axis=0, tiled=True
    ).reshape(groups * SLOTS, -1)
    chip = jnp.concatenate([picked, swap(picked, 1)])
    plane = jnp.concatenate([chip] + [swap(chip, bits) for bits in (2, 4, 6)])
    levels = [plane] + [swap(plane, bits) for bits in range(PLANE, groups, PLANE)]
    observed = pl.pallas_call(
        compact_kernel,
        out_shape=jax.ShapeDtypeStruct((count, width), jnp.bfloat16),
        in_specs=[VMEM] * 2,
        out_specs=VMEM,
        compiler_params=room(8),
        name="compact",
    )(order, got)
    def invert(panel_range, sources, out_shape):
        return pl.pallas_call(
            functools.partial(invert_kernel, panel_range),
            out_shape=out_shape,
            in_specs=[VMEM] * len(sources),
            out_specs=VMEM,
            scratch_shapes=[pltpu.VMEM((count, count), jnp.float32)],
            cost_estimate=pl.CostEstimate(
                flops=200 * len(panel_range) * count**3,
                bytes_accessed=4 * count * count,
                transcendentals=count,
            ),
            compiler_params=room(4),
            name="invert",
        )(*sources)

    def update(inverse, flips, pieces, before):
        more = () if before is None else (before,)
        return pl.pallas_call(
            functools.partial(update_kernel, width, flips),
            out_shape=jax.ShapeDtypeStruct(slab.shape, jnp.bfloat16),
            in_specs=[VMEM] * (3 + len(pieces)) + [HBM] * len(more),
            out_specs=HBM,
            scratch_shapes=[
                pltpu.VMEM((len(flips), rows, width), jnp.bfloat16),
                pltpu.SemaphoreType.DMA((len(flips),)),
            ],
            input_output_aliases={3 + len(pieces): 0} if more else {},
            compiler_params=room(12),
            name="update",
        )(inverse, cross, slab, *pieces, *more)

    by = {0: observed, 1: swap(observed, 1)}
    by.update({group: swap(observed, bit) for bit, group in ((2, 2), (4, 4), (8, 6))})
    panels, early = count // 8, 3 * count // 32
    midway = invert(
        range(early),
        (cross_order, diagonal, *levels),
        jax.ShapeDtypeStruct((count, count), jnp.float32),
    )
    arrived, midway = lax.optimization_barrier(([by[g] for g in (2, 4, 6)], midway))
    for group, piece in zip((2, 4, 6), arrived):
        by[group] = piece
        by[group + 1] = swap(piece, 1)
    inverse = invert(
        range(early, panels), (midway,), jax.ShapeDtypeStruct((PARTS * count, count), jnp.bfloat16)
    )
    flips = tuple(range(PLANE))
    return update(inverse, flips, [by[f] for f in flips], None)


def solution(mesh):
    plane = mesh.shape["cols"] == 1 and mesh.shape["rows"] == 4 * PLANE
    return jax.shard_map(
        plane_body if plane else general_body,
        mesh=mesh,
        in_specs=(P("rows", "cols"), P("rows", "cols"), P(), P()),
        out_specs=P("rows", "cols"),
        check_vma=False,
    )
```

```python
import functools

import jax
import jax.numpy as jnp
from jax import lax
from jax.experimental import pallas as pl
from jax.experimental.pallas import tpu as pltpu
from jax.sharding import PartitionSpec as P

CAP = 12
SLOTS = 16
PLANE = 8
PARTS = 3
VMEM = pl.BlockSpec(memory_space=pltpu.VMEM)
HBM = pl.BlockSpec(memory_space=pltpu.HBM)
MIB = 1 << 20


def room(mib):
    return pltpu.CompilerParams(vmem_limit_bytes=mib * MIB)


def dot32(a, b):
    return jnp.dot(a, b, preferred_element_type=jnp.float32)


def solve_gain(factor, right_side):
    forward = lax.linalg.triangular_solve(factor, right_side, left_side=True, lower=True)
    return lax.linalg.triangular_solve(
        factor, forward, left_side=True, lower=True, transpose_a=True
    )


def make_factor(picked_half, noise):
    picked = lax.all_gather(picked_half, "cols", axis=1, tiled=True).astype(jnp.float32)
    innovation = 0.5 * (picked + picked.T) + jnp.diag(noise)
    return jnp.linalg.cholesky(innovation)


def general_body(slab, cross, obs_index, noise):
    row_count = slab.shape[0]
    groups = lax.axis_size("rows")
    owners = obs_index // row_count
    local_row = obs_index % row_count
    owner_hit = (owners[:, None] == jnp.arange(groups, dtype=jnp.int32)[None, :]).astype(jnp.int32)
    before = jnp.cumsum(owner_hit, axis=0) - owner_hit
    slot_rank = jnp.sum(before * owner_hit, axis=1)
    mine = owners == lax.axis_index("rows")
    slot_hit = (
        mine[:, None] & (slot_rank[:, None] == jnp.arange(CAP, dtype=jnp.int32)[None, :])
    ).astype(jnp.bfloat16)
    row_hit = (local_row[:, None] == jnp.arange(row_count, dtype=jnp.int32)[None, :]).astype(
        jnp.bfloat16
    )
    selector = dot32(slot_hit.T, row_hit).astype(jnp.bfloat16)
    packed_cross = dot32(selector, cross).astype(jnp.bfloat16)
    packed_slab = dot32(selector, slab).astype(jnp.bfloat16)
    placed = owners * CAP + slot_rank
    all_cross, all_slab = (
        lax.all_gather(packed_cross, "rows", axis=0, tiled=True),
        lax.all_gather(packed_slab, "rows", axis=0, tiled=True),
    )
    factor = make_factor(all_cross[placed], noise)
    observed = all_slab[placed].astype(jnp.float32)
    gain = solve_gain(factor, observed).astype(jnp.bfloat16)
    update = dot32(lax.all_gather(cross, "cols", axis=1, tiled=True), gain)
    return (slab.astype(jnp.float32) - update).astype(jnp.bfloat16)


def spread_index(obs_ref, rows):
    count = obs_ref.shape[1]
    along = jnp.broadcast_to(obs_ref[...], (count, count))
    down = along.astype(jnp.float32).T.astype(jnp.int32)
    earlier_row = lax.broadcasted_iota(jnp.int32, (count, count), 0)
    earlier_col = lax.broadcasted_iota(jnp.int32, (count, count), 1)
    same = along // rows == down // rows
    rank_along = jnp.sum(
        jnp.where(same & (earlier_row < earlier_col), 1.0, 0.0), axis=0, keepdims=True
    ).astype(jnp.int32)
    rank_down = jnp.sum(
        jnp.where(same & (earlier_col < earlier_row), 1.0, 0.0), axis=1, keepdims=True
    ).astype(jnp.int32)
    return along, down, rank_along, rank_down


def column_group(device):
    return (device % PLANE) ^ (6 * ((device // PLANE) % 2))


def pick_kernel(
    groups, width, obs_hbm, slab_hbm, cross_hbm, out_hbm, picked_hbm, obs_ref, slab, cross, out, picked, sem, out_sem
):
    rows, count = slab.shape[0], obs_ref.shape[1]
    half = slab.shape[1] // 2

    def fetch(source, target, index):
        copy = pltpu.make_async_copy(source, target, sem.at[index])
        copy.start()
        return copy

    got_obs = fetch(obs_hbm, obs_ref, 0)
    got_cross = fetch(cross_hbm, cross, 1)
    got_slab = [
        fetch(slab_hbm.at[:, i * half : (i + 1) * half], slab.at[:, i * half : (i + 1) * half], 2 + i)
        for i in range(2)
    ]
    me = lax.axis_index("rows")
    got_obs.wait()
    along, down, rank, _ = spread_index(obs_ref, rows)
    picks = 4 * SLOTS
    slot = lax.broadcasted_iota(jnp.int32, (picks, count), 0)
    within, part = slot % SLOTS, slot // SLOTS
    wanted = jnp.where(
        part == 0,
        jnp.where(within < CAP, within, -1),
        jnp.where(within >= CAP, 4 * (part - 1) + within - CAP, -1),
    )
    mine = (along[:1] // rows) == me
    hit = jnp.where(mine & (rank == wanted), 1.0, 0.0).astype(jnp.bfloat16)
    local = lax.broadcasted_iota(jnp.int32, (count, rows), 1) == down[:, :rows] % rows
    selector = dot32(hit, jnp.where(local, 1.0, 0.0).astype(jnp.bfloat16)).astype(jnp.bfloat16)
    got_cross.wait()
    picked[...] = dot32(selector[:SLOTS], cross[...]).astype(jnp.bfloat16)
    lanes = width // 4
    sent = [pltpu.make_async_copy(picked, picked_hbm, out_sem.at[0])]
    sent[0].start()
    for group in range(PLANE):
        if group % 4 == 0:
            got_slab[group // 4].wait()
        got = dot32(selector, slab[:, group * width : (group + 1) * width])
        tail = got[:, 3 * lanes :]
        out[group * SLOTS : (group + 1) * SLOTS, :] = jnp.concatenate(
            [
                (
                    got[:SLOTS, t * lanes : (t + 1) * lanes]
                    + tail[(t + 1) * SLOTS : (t + 2) * SLOTS]
                ).astype(jnp.bfloat16)
                for t in range(3)
            ],
            axis=1,
        )
        if group % 2:
            source = out.at[(group - 1) * SLOTS : (group + 1) * SLOTS]
            for level in range(groups // PLANE):
                to = (level * PLANE + column_group(level * PLANE + group - 1)) * SLOTS
                copy = pltpu.make_async_copy(
                    source, out_hbm.at[to : to + 2 * SLOTS], out_sem.at[len(sent)]
                )
                copy.start()
                sent.append(copy)
    for copy in sent:
        copy.wait()


def order_kernel(rows, obs_ref, noise_ref, order_ref, cross_order_ref, diagonal_ref):
    count, slots = obs_ref.shape[1], order_ref.shape[1]
    _, down, _, rank = spread_index(obs_ref, rows)
    owner = down[:, :1] // rows
    lane = lax.broadcasted_iota(jnp.int32, (count, slots), 1)
    within, device = lane % SLOTS, lane // SLOTS

    def one_hot(hit):
        return jnp.where(hit, 1.0, 0.0).astype(jnp.bfloat16)

    owned = owner == device
    order_ref[:count, :] = one_hot(owned & (rank == within))
    for t in range(3):
        hit = (within >= CAP) & (rank == within + (4 * t - CAP))
        order_ref[(t + 1) * count : (t + 2) * count, :] = one_hot(owned & hit)
    apart = owner ^ lax.axis_index("rows")
    cross_order_ref[...] = one_hot((apart == device) & (rank == within))
    square = (count, count)
    on = lax.broadcasted_iota(jnp.int32, square, 0) == lax.broadcasted_iota(jnp.int32, square, 1)
    diagonal_ref[...] = jnp.where(on, noise_ref[...], 0.0)


def compact_kernel(order_ref, got_ref, observed_ref):
    count = observed_ref.shape[0]
    lanes = got_ref.shape[1] // 3
    head = dot32(order_ref[:count, :], got_ref[...])
    tail = jnp.zeros((count, lanes), jnp.float32)
    for t in range(3):
        hit = order_ref[(t + 1) * count : (t + 2) * count, :]
        tail += dot32(hit, got_ref[:, t * lanes : (t + 1) * lanes])
    observed_ref[:, : 3 * lanes] = head.astype(jnp.bfloat16)
    observed_ref[:, 3 * lanes :] = tail.astype(jnp.bfloat16)


def innovation_of(order_ref, diagonal_ref, *pieces):
    span = pieces[0].shape[0]
    picked = sum(
        dot32(order_ref[:, i * span : (i + 1) * span], piece[...])
        for i, piece in enumerate(pieces)
    )
    return 0.5 * (picked + picked.T) + diagonal_ref[...]


def tree_sum(terms):
    while len(terms) > 1:
        terms = [x + y for x, y in zip(terms[::2], terms[1::2])]
    return terms[0]


def sweep(e, step):
    def at(i, k):
        return max(i, k), min(i, k)

    for k in range(0, step, 2):
        a, b, c = e[k, k], e[k + 1, k], e[k + 1, k + 1]
        over = 1.0 / (a * c - b * b)
        pa, pb, pc = c * over, -b * over, a * over
        others = [i for i in range(step) if i not in (k, k + 1)]
        u = {i: e[at(i, k)] for i in others}
        v = {i: e[at(i, k + 1)] for i in others}
        su = {i: u[i] * pa + v[i] * pb for i in others}
        sv = {i: u[i] * pb + v[i] * pc for i in others}
        for i in others:
            for j in others:
                if j <= i:
                    e[i, j] = e[i, j] - (su[i] * u[j] + sv[i] * v[j])
        for i in others:
            e[at(i, k)], e[at(i, k + 1)] = su[i], sv[i]
        e[k, k], e[k + 1, k], e[k + 1, k + 1] = -pa, -pb, -pc


def invert_kernel(panel_range, sources, *refs):
    inputs, outputs, (spread_ref,) = refs[:sources], refs[sources:-1], refs[-1:]
    step = 8
    first, stop = panel_range[0], panel_range[-1] + 1
    if first == 0:
        inn = innovation_of(*inputs)
        state_ref, solved_ref = outputs
        size = inn.shape[0]
        state_ref[...] = inn
        given = state_ref
    else:
        given, solved_before = inputs
        out_ref, state_ref, solved_ref = outputs
        size = given.shape[0]
        done = first * step
        state_ref[:done, :] = given[:done, :]
        solved_ref[:done, :] = solved_before[:done, :]
    full, panels = (step, size), size // step
    m = {i: given[i * step : (i + 1) * step, :] for i in range(first, panels)}
    sub = lax.broadcasted_iota(jnp.int32, full, 0)
    lane = lax.broadcasted_iota(jnp.int32, full, 1)
    for p in panel_range:
        at, base = p * step, (p % 2) * (step + 1)
        row = m[p]
        for k in range(step):
            spread_ref[base + k] = jnp.broadcast_to(row[:, at + k : at + k + 1], full)
        e = {
            (i, k): jnp.broadcast_to(spread_ref[base + k, i : i + 1, :], full)
            for i in range(step)
            for k in range(i + 1)
        }
        inside = (lane >= at) & (lane < at + step)
        known = lane < at + step
        unit = jnp.where(inside, jnp.where(lane == sub + at, 1.0, 0.0), row)
        spread_ref[base + step] = unit
        sweep(e, step)
        rows_b = [
            jnp.broadcast_to(spread_ref[base + step, k : k + 1, :], full) for k in range(step)
        ]
        q = [
            tree_sum([e[max(i, k), min(i, k)] * rows_b[k] for k in range(step)])
            for i in range(step)
        ]
        for i in range(p + 1, panels):
            terms = [
                jnp.broadcast_to(m[i][:, at + k : at + k + 1], full) * q[k] for k in range(step)
            ]
            m[i] = jnp.where(inside, 0.0, m[i]) + tree_sum(terms)
        solved = q[0]
        for i in range(1, step):
            solved = jnp.where(sub == i, q[i], solved)
        state_ref[at : at + step, :] = jnp.where(known, unit, 0.0)
        solved_ref[at : at + step, :] = jnp.where(known, -solved, 0.0)
    if stop < panels:
        for i in range(stop, panels):
            state_ref[i * step : (i + 1) * step, :] = m[i]
        solved_ref[stop * step :, :] = jnp.zeros((size - stop * step, size), jnp.float32)
        return
    x = lax.dot_general(
        state_ref[...],
        solved_ref[...],
        (((0,), (0,)), ((), ())),
        precision=lax.Precision.HIGHEST,
        preferred_element_type=jnp.float32,
    )
    for part in range(PARTS):
        piece = x.astype(jnp.bfloat16)
        out_ref[part * size : (part + 1) * size, :] = piece
        x = x - piece.astype(jnp.float32)


def update_kernel(width, flips, inverse_ref, cross_ref, slab_ref, *refs):
    pieces, (out_ref, held, sem) = refs[: len(flips)], refs[-3:]
    place = column_group(lax.axis_index("rows"))
    cross = cross_ref[...]
    size = cross.shape[1]
    inverse = jnp.concatenate(
        [inverse_ref[t * size : (t + 1) * size] for t in range(PARTS)], axis=1
    )
    copies, gains = [], []
    for piece in pieces:
        gains.append(
            dot32(inverse, jnp.concatenate([piece[...]] * PARTS, axis=0)).astype(jnp.bfloat16)
        )
    for index, flip in enumerate(flips):
        at = pl.multiple_of((place ^ flip) * width, width)
        new = slab_ref[:, pl.ds(at, width)].astype(jnp.float32) - dot32(cross, gains[index])
        held[index] = new.astype(jnp.bfloat16)
        copy = pltpu.make_async_copy(
            held.at[index], out_ref.at[:, pl.ds(at, width)], sem.at[index]
        )
        copy.start()
        copies.append(copy)
    for copy in copies:
        copy.wait()


def plane_body(slab, cross, obs_index, noise):
    groups = lax.axis_size("rows")
    rows, columns = slab.shape
    count = cross.shape[1]
    width = columns // PLANE
    obs = obs_index.reshape(1, count)
    packed, picked = pl.pallas_call(
        functools.partial(pick_kernel, groups, width),
        out_shape=(
            jax.ShapeDtypeStruct((groups * SLOTS, 3 * width // 4), jnp.bfloat16),
            jax.ShapeDtypeStruct((SLOTS, count), jnp.bfloat16),
        ),
        in_specs=[HBM] * 3,
        out_specs=(HBM, HBM),
        scratch_shapes=[
            pltpu.VMEM((1, count), jnp.int32),
            pltpu.VMEM(slab.shape, jnp.bfloat16),
            pltpu.VMEM(cross.shape, jnp.bfloat16),
            pltpu.VMEM((PLANE * SLOTS, 3 * width // 4), jnp.bfloat16),
            pltpu.VMEM((SLOTS, count), jnp.bfloat16),
            pltpu.SemaphoreType.DMA((4,)),
            pltpu.SemaphoreType.DMA((1 + groups // 2,)),
        ],
        compiler_params=room(56),
        name="pick",
    )(obs, slab, cross)
    order, cross_order, diagonal = pl.pallas_call(
        functools.partial(order_kernel, rows),
        out_shape=(
            jax.ShapeDtypeStruct((4 * count, groups * SLOTS), jnp.bfloat16),
            jax.ShapeDtypeStruct((count, groups * SLOTS), jnp.bfloat16),
            jax.ShapeDtypeStruct((count, count), jnp.float32),
        ),
        in_specs=[VMEM] * 2,
        out_specs=(VMEM,) * 3,
        cost_estimate=pl.CostEstimate(
            flops=1000 * count**3, bytes_accessed=4 * count * count, transcendentals=0
        ),
        compiler_params=room(8),
        name="order",
    )(obs, noise.reshape(1, count))

    def swap(value, bit):
        return lax.ppermute(value, "rows", [(i, i ^ bit) for i in range(groups)])

    got = lax.all_to_all(
        packed.reshape(groups, SLOTS, -1), "rows", split_axis=0, concat_axis=0, tiled=True
    ).reshape(groups * SLOTS, -1)
    chip = jnp.concatenate([picked, swap(picked, 1)])
    plane = jnp.concatenate([chip] + [swap(chip, bits) for bits in (2, 4, 6)])
    levels = [plane] + [swap(plane, bits) for bits in range(PLANE, groups, PLANE)]
    observed = pl.pallas_call(
        compact_kernel,
        out_shape=jax.ShapeDtypeStruct((count, width), jnp.bfloat16),
        in_specs=[VMEM] * 2,
        out_specs=VMEM,
        compiler_params=room(8),
        name="compact",
    )(order, got)
    square = jax.ShapeDtypeStruct((count, count), jnp.float32)

    def invert(panel_range, sources):
        first = panel_range[0] == 0
        parts = jax.ShapeDtypeStruct((PARTS * count, count), jnp.bfloat16)
        return pl.pallas_call(
            functools.partial(invert_kernel, panel_range, len(sources)),
            out_shape=(square, square) if first else parts,
            in_specs=[VMEM] * len(sources),
            out_specs=(VMEM, VMEM) if first else VMEM,
            scratch_shapes=([] if first else [pltpu.VMEM((count, count), jnp.float32)] * 2)
            + [pltpu.VMEM((18, 8, count), jnp.float32)],
            cost_estimate=pl.CostEstimate(
                flops=200 * len(panel_range) * count**3,
                bytes_accessed=4 * count * count,
                transcendentals=count,
            ),
            compiler_params=room(4),
            name="invert",
        )(*sources)

    def update(inverse, flips, pieces, before):
        more = () if before is None else (before,)
        return pl.pallas_call(
            functools.partial(update_kernel, width, flips),
            out_shape=jax.ShapeDtypeStruct(slab.shape, jnp.bfloat16),
            in_specs=[VMEM] * (3 + len(pieces)) + [HBM] * len(more),
            out_specs=HBM,
            scratch_shapes=[
                pltpu.VMEM((len(flips), rows, width), jnp.bfloat16),
                pltpu.SemaphoreType.DMA((len(flips),)),
            ],
            input_output_aliases={3 + len(pieces): 0} if more else {},
            compiler_params=room(12),
            name="update",
        )(inverse, cross, slab, *pieces, *more)

    by = {0: observed, 1: swap(observed, 1)}
    by.update({group: swap(observed, bit) for bit, group in ((2, 2), (4, 4), (8, 6))})
    panels, early = count // 8, 12 * count // 128
    midway = invert(range(early), (cross_order, diagonal, *levels))
    arrived, midway = lax.optimization_barrier(([by[g] for g in (2, 4, 6)], midway))
    for group, piece in zip((2, 4, 6), arrived):
        by[group] = piece
        by[group + 1] = swap(piece, 1)
    inverse = invert(range(early, panels), tuple(midway))
    flips = tuple(range(PLANE))
    return update(inverse, flips, [by[f] for f in flips], None)


def solution(mesh):
    plane = mesh.shape["cols"] == 1 and mesh.shape["rows"] == 4 * PLANE
    return jax.shard_map(
        plane_body if plane else general_body,
        mesh=mesh,
        in_specs=(P("rows", "cols"), P("rows", "cols"), P(), P()),
        out_specs=P("rows", "cols"),
        check_vma=False,
    )
```

```python
import functools

import jax
import jax.numpy as jnp
from jax import lax
from jax.experimental import pallas as pl
from jax.experimental.pallas import tpu as pltpu
from jax.sharding import PartitionSpec as P

CAP = 12
SLOTS = 16
PLANE = 8
PARTS = 3
VMEM = pl.BlockSpec(memory_space=pltpu.VMEM)
HBM = pl.BlockSpec(memory_space=pltpu.HBM)
MIB = 1 << 20


def room(mib):
    return pltpu.CompilerParams(vmem_limit_bytes=mib * MIB)


def dot32(a, b):
    return jnp.dot(a, b, preferred_element_type=jnp.float32)


def solve_gain(factor, right_side):
    forward = lax.linalg.triangular_solve(factor, right_side, left_side=True, lower=True)
    return lax.linalg.triangular_solve(
        factor, forward, left_side=True, lower=True, transpose_a=True
    )


def make_factor(picked_half, noise):
    picked = lax.all_gather(picked_half, "cols", axis=1, tiled=True).astype(jnp.float32)
    innovation = 0.5 * (picked + picked.T) + jnp.diag(noise)
    return jnp.linalg.cholesky(innovation)


def general_body(slab, cross, obs_index, noise):
    row_count = slab.shape[0]
    groups = lax.axis_size("rows")
    owners = obs_index // row_count
    local_row = obs_index % row_count
    owner_hit = (owners[:, None] == jnp.arange(groups, dtype=jnp.int32)[None, :]).astype(jnp.int32)
    before = jnp.cumsum(owner_hit, axis=0) - owner_hit
    slot_rank = jnp.sum(before * owner_hit, axis=1)
    mine = owners == lax.axis_index("rows")
    slot_hit = (
        mine[:, None] & (slot_rank[:, None] == jnp.arange(CAP, dtype=jnp.int32)[None, :])
    ).astype(jnp.bfloat16)
    row_hit = (local_row[:, None] == jnp.arange(row_count, dtype=jnp.int32)[None, :]).astype(
        jnp.bfloat16
    )
    selector = dot32(slot_hit.T, row_hit).astype(jnp.bfloat16)
    packed_cross = dot32(selector, cross).astype(jnp.bfloat16)
    packed_slab = dot32(selector, slab).astype(jnp.bfloat16)
    placed = owners * CAP + slot_rank
    all_cross, all_slab = (
        lax.all_gather(packed_cross, "rows", axis=0, tiled=True),
        lax.all_gather(packed_slab, "rows", axis=0, tiled=True),
    )
    factor = make_factor(all_cross[placed], noise)
    observed = all_slab[placed].astype(jnp.float32)
    gain = solve_gain(factor, observed).astype(jnp.bfloat16)
    update = dot32(lax.all_gather(cross, "cols", axis=1, tiled=True), gain)
    return (slab.astype(jnp.float32) - update).astype(jnp.bfloat16)


def spread_index(obs_ref, rows):
    count = obs_ref.shape[1]
    along = jnp.broadcast_to(obs_ref[...], (count, count))
    down = along.astype(jnp.float32).T.astype(jnp.int32)
    earlier_row = lax.broadcasted_iota(jnp.int32, (count, count), 0)
    earlier_col = lax.broadcasted_iota(jnp.int32, (count, count), 1)
    same = along // rows == down // rows
    rank_along = jnp.sum(
        jnp.where(same & (earlier_row < earlier_col), 1.0, 0.0), axis=0, keepdims=True
    ).astype(jnp.int32)
    rank_down = jnp.sum(
        jnp.where(same & (earlier_col < earlier_row), 1.0, 0.0), axis=1, keepdims=True
    ).astype(jnp.int32)
    return along, down, rank_along, rank_down


def column_group(device):
    return (device % PLANE) ^ (6 * ((device // PLANE) % 2))


def pick_kernel(
    groups, width, obs_hbm, slab_hbm, cross_hbm, out_hbm, picked_hbm, obs_ref, slab, cross, out, picked, sem, out_sem
):
    rows, count = slab.shape[0], obs_ref.shape[1]
    half = slab.shape[1] // 2

    def fetch(source, target, index):
        copy = pltpu.make_async_copy(source, target, sem.at[index])
        copy.start()
        return copy

    got_obs = fetch(obs_hbm, obs_ref, 0)
    got_cross = fetch(cross_hbm, cross, 1)
    got_slab = [
        fetch(slab_hbm.at[:, i * half : (i + 1) * half], slab.at[:, i * half : (i + 1) * half], 2 + i)
        for i in range(2)
    ]
    me = lax.axis_index("rows")
    got_obs.wait()
    along, down, rank, _ = spread_index(obs_ref, rows)
    picks = 4 * SLOTS
    slot = lax.broadcasted_iota(jnp.int32, (picks, count), 0)
    within, part = slot % SLOTS, slot // SLOTS
    wanted = jnp.where(
        part == 0,
        jnp.where(within < CAP, within, -1),
        jnp.where(within >= CAP, 4 * (part - 1) + within - CAP, -1),
    )
    mine = (along[:1] // rows) == me
    hit = jnp.where(mine & (rank == wanted), 1.0, 0.0).astype(jnp.bfloat16)
    local = lax.broadcasted_iota(jnp.int32, (count, rows), 1) == down[:, :rows] % rows
    selector = dot32(hit, jnp.where(local, 1.0, 0.0).astype(jnp.bfloat16)).astype(jnp.bfloat16)
    got_cross.wait()
    picked[...] = dot32(selector[:SLOTS], cross[...]).astype(jnp.bfloat16)
    lanes = width // 4
    sent = [pltpu.make_async_copy(picked, picked_hbm, out_sem.at[0])]
    sent[0].start()
    for group in range(PLANE):
        if group % 4 == 0:
            got_slab[group // 4].wait()
        got = dot32(selector, slab[:, group * width : (group + 1) * width])
        tail = got[:, 3 * lanes :]
        out[group * SLOTS : (group + 1) * SLOTS, :] = jnp.concatenate(
            [
                (
                    got[:SLOTS, t * lanes : (t + 1) * lanes]
                    + tail[(t + 1) * SLOTS : (t + 2) * SLOTS]
                ).astype(jnp.bfloat16)
                for t in range(3)
            ],
            axis=1,
        )
        if group % 2:
            source = out.at[(group - 1) * SLOTS : (group + 1) * SLOTS]
            for level in range(groups // PLANE):
                to = (level * PLANE + column_group(level * PLANE + group - 1)) * SLOTS
                copy = pltpu.make_async_copy(
                    source, out_hbm.at[to : to + 2 * SLOTS], out_sem.at[len(sent)]
                )
                copy.start()
                sent.append(copy)
    for copy in sent:
        copy.wait()


def order_kernel(rows, obs_ref, noise_ref, order_ref, cross_order_ref, diagonal_ref):
    count, slots = obs_ref.shape[1], order_ref.shape[1]
    _, down, _, rank = spread_index(obs_ref, rows)
    owner = down[:, :1] // rows
    lane = lax.broadcasted_iota(jnp.int32, (count, slots), 1)
    within, device = lane % SLOTS, lane // SLOTS

    def one_hot(hit):
        return jnp.where(hit, 1.0, 0.0).astype(jnp.bfloat16)

    owned = owner == device
    order_ref[:count, :] = one_hot(owned & (rank == within))
    for t in range(3):
        hit = (within >= CAP) & (rank == within + (4 * t - CAP))
        order_ref[(t + 1) * count : (t + 2) * count, :] = one_hot(owned & hit)
    apart = owner ^ lax.axis_index("rows")
    cross_order_ref[...] = one_hot((apart == device) & (rank == within))
    square = (count, count)
    on = lax.broadcasted_iota(jnp.int32, square, 0) == lax.broadcasted_iota(jnp.int32, square, 1)
    diagonal_ref[...] = jnp.where(on, noise_ref[...], 0.0)


def compact_kernel(order_ref, got_ref, observed_ref):
    count = observed_ref.shape[0]
    lanes = got_ref.shape[1] // 3
    head = dot32(order_ref[:count, :], got_ref[...])
    tail = jnp.zeros((count, lanes), jnp.float32)
    for t in range(3):
        hit = order_ref[(t + 1) * count : (t + 2) * count, :]
        tail += dot32(hit, got_ref[:, t * lanes : (t + 1) * lanes])
    observed_ref[:, : 3 * lanes] = head.astype(jnp.bfloat16)
    observed_ref[:, 3 * lanes :] = tail.astype(jnp.bfloat16)


def innovation_of(order_ref, diagonal_ref, *pieces):
    span = pieces[0].shape[0]
    picked = sum(
        dot32(order_ref[:, i * span : (i + 1) * span], piece[...])
        for i, piece in enumerate(pieces)
    )
    return 0.5 * (picked + picked.T) + diagonal_ref[...]


def tree_sum(terms):
    while len(terms) > 1:
        terms = [x + y for x, y in zip(terms[::2], terms[1::2])]
    return terms[0]


def sweep(e, step):
    def at(i, k):
        return max(i, k), min(i, k)

    for k in range(0, step, 2):
        a, b, c = e[k, k], e[k + 1, k], e[k + 1, k + 1]
        over = 1.0 / (a * c - b * b)
        pa, pb, pc = c * over, -b * over, a * over
        others = [i for i in range(step) if i not in (k, k + 1)]
        u = {i: e[at(i, k)] for i in others}
        v = {i: e[at(i, k + 1)] for i in others}
        su = {i: u[i] * pa + v[i] * pb for i in others}
        sv = {i: u[i] * pb + v[i] * pc for i in others}
        for i in others:
            for j in others:
                if j <= i:
                    e[i, j] = e[i, j] - (su[i] * u[j] + sv[i] * v[j])
        for i in others:
            e[at(i, k)], e[at(i, k + 1)] = su[i], sv[i]
        e[k, k], e[k + 1, k], e[k + 1, k + 1] = -pa, -pb, -pc


def gain_of(inverse_parts, observed):
    return dot32(inverse_parts, jnp.concatenate([observed] * PARTS, axis=0)).astype(jnp.bfloat16)


def invert_kernel(panel_range, sources, *refs):
    inputs, outputs, (spread_ref,) = refs[:sources], refs[sources:-1], refs[-1:]
    step = 8
    first, stop = panel_range[0], panel_range[-1] + 1
    if first == 0:
        inn = innovation_of(*inputs)
        state_ref, solved_ref = outputs
        size = inn.shape[0]
        state_ref[...] = inn
        given = state_ref
    else:
        given, solved_before = inputs[:2]
        out_ref, gain_ref, state_ref, solved_ref = outputs
        size = given.shape[0]
        done = first * step
        state_ref[:done, :] = given[:done, :]
        solved_ref[:done, :] = solved_before[:done, :]
    full, panels = (step, size), size // step
    m = {i: given[i * step : (i + 1) * step, :] for i in range(first, panels)}
    sub = lax.broadcasted_iota(jnp.int32, full, 0)
    lane = lax.broadcasted_iota(jnp.int32, full, 1)
    for p in panel_range:
        at, base = p * step, (p % 2) * (step + 1)
        row = m[p]
        for k in range(step):
            spread_ref[base + k] = jnp.broadcast_to(row[:, at + k : at + k + 1], full)
        e = {
            (i, k): jnp.broadcast_to(spread_ref[base + k, i : i + 1, :], full)
            for i in range(step)
            for k in range(i + 1)
        }
        inside = (lane >= at) & (lane < at + step)
        known = lane < at + step
        unit = jnp.where(inside, jnp.where(lane == sub + at, 1.0, 0.0), row)
        spread_ref[base + step] = unit
        sweep(e, step)
        rows_b = [
            jnp.broadcast_to(spread_ref[base + step, k : k + 1, :], full) for k in range(step)
        ]
        q = [
            tree_sum([e[max(i, k), min(i, k)] * rows_b[k] for k in range(step)])
            for i in range(step)
        ]
        for i in range(p + 1, panels):
            terms = [
                jnp.broadcast_to(m[i][:, at + k : at + k + 1], full) * q[k] for k in range(step)
            ]
            m[i] = jnp.where(inside, 0.0, m[i]) + tree_sum(terms)
        solved = q[0]
        for i in range(1, step):
            solved = jnp.where(sub == i, q[i], solved)
        state_ref[at : at + step, :] = jnp.where(known, unit, 0.0)
        solved_ref[at : at + step, :] = jnp.where(known, -solved, 0.0)
    if stop < panels:
        for i in range(stop, panels):
            state_ref[i * step : (i + 1) * step, :] = m[i]
        solved_ref[stop * step :, :] = jnp.zeros((size - stop * step, size), jnp.float32)
        return
    x = lax.dot_general(
        state_ref[...],
        solved_ref[...],
        (((0,), (0,)), ((), ())),
        precision=lax.Precision.HIGHEST,
        preferred_element_type=jnp.float32,
    )
    parts = []
    for part in range(PARTS):
        piece = x.astype(jnp.bfloat16)
        out_ref[part * size : (part + 1) * size, :] = piece
        x = x - piece.astype(jnp.float32)
        parts.append(piece)
    for index, piece in enumerate(inputs[2:]):
        gain_ref[index] = gain_of(jnp.concatenate(parts, axis=1), piece[...])


def update_kernel(width, flips, inverse_ref, gain_ref, cross_ref, slab_ref, *refs):
    pieces, (out_ref, held, sem) = refs[:-3], refs[-3:]
    place = column_group(lax.axis_index("rows"))
    cross = cross_ref[...]
    size = cross.shape[1]
    inverse = jnp.concatenate(
        [inverse_ref[t * size : (t + 1) * size] for t in range(PARTS)], axis=1
    )
    copies = []
    ready = gain_ref.shape[0]
    gains = [gain_ref[i] for i in range(ready)]
    for index, flip in enumerate(flips):
        if index == ready:
            gains += [gain_of(inverse, piece[...]) for piece in pieces]
        at = pl.multiple_of((place ^ flip) * width, width)
        new = slab_ref[:, pl.ds(at, width)].astype(jnp.float32) - dot32(cross, gains[index])
        held[index] = new.astype(jnp.bfloat16)
        copy = pltpu.make_async_copy(
            held.at[index], out_ref.at[:, pl.ds(at, width)], sem.at[index]
        )
        copy.start()
        copies.append(copy)
    for copy in copies:
        copy.wait()


def plane_body(slab, cross, obs_index, noise):
    groups = lax.axis_size("rows")
    rows, columns = slab.shape
    count = cross.shape[1]
    width = columns // PLANE
    obs = obs_index.reshape(1, count)
    packed, picked = pl.pallas_call(
        functools.partial(pick_kernel, groups, width),
        out_shape=(
            jax.ShapeDtypeStruct((groups * SLOTS, 3 * width // 4), jnp.bfloat16),
            jax.ShapeDtypeStruct((SLOTS, count), jnp.bfloat16),
        ),
        in_specs=[HBM] * 3,
        out_specs=(HBM, HBM),
        scratch_shapes=[
            pltpu.VMEM((1, count), jnp.int32),
            pltpu.VMEM(slab.shape, jnp.bfloat16),
            pltpu.VMEM(cross.shape, jnp.bfloat16),
            pltpu.VMEM((PLANE * SLOTS, 3 * width // 4), jnp.bfloat16),
            pltpu.VMEM((SLOTS, count), jnp.bfloat16),
            pltpu.SemaphoreType.DMA((4,)),
            pltpu.SemaphoreType.DMA((1 + groups // 2,)),
        ],
        compiler_params=room(56),
        name="pick",
    )(obs, slab, cross)
    order, cross_order, diagonal = pl.pallas_call(
        functools.partial(order_kernel, rows),
        out_shape=(
            jax.ShapeDtypeStruct((4 * count, groups * SLOTS), jnp.bfloat16),
            jax.ShapeDtypeStruct((count, groups * SLOTS), jnp.bfloat16),
            jax.ShapeDtypeStruct((count, count), jnp.float32),
        ),
        in_specs=[VMEM] * 2,
        out_specs=(VMEM,) * 3,
        cost_estimate=pl.CostEstimate(
            flops=1000 * count**3, bytes_accessed=4 * count * count, transcendentals=0
        ),
        compiler_params=room(8),
        name="order",
    )(obs, noise.reshape(1, count))

    def swap(value, bit):
        return lax.ppermute(value, "rows", [(i, i ^ bit) for i in range(groups)])

    got = lax.all_to_all(
        packed.reshape(groups, SLOTS, -1), "rows", split_axis=0, concat_axis=0, tiled=True
    ).reshape(groups * SLOTS, -1)
    chip = jnp.concatenate([picked, swap(picked, 1)])
    plane = jnp.concatenate([chip] + [swap(chip, bits) for bits in (2, 4, 6)])
    levels = [plane] + [swap(plane, bits) for bits in range(PLANE, groups, PLANE)]
    observed = pl.pallas_call(
        compact_kernel,
        out_shape=jax.ShapeDtypeStruct((count, width), jnp.bfloat16),
        in_specs=[VMEM] * 2,
        out_specs=VMEM,
        compiler_params=room(8),
        name="compact",
    )(order, got)
    square = jax.ShapeDtypeStruct((count, count), jnp.float32)

    def invert(panel_range, sources):
        first = panel_range[0] == 0
        parts = jax.ShapeDtypeStruct((PARTS * count, count), jnp.bfloat16)
        gains = jax.ShapeDtypeStruct((len(sources) - 2, count, width), jnp.bfloat16)
        return pl.pallas_call(
            functools.partial(invert_kernel, panel_range, len(sources)),
            out_shape=(square, square) if first else (parts, gains),
            in_specs=[VMEM] * len(sources),
            out_specs=(VMEM, VMEM),
            scratch_shapes=([] if first else [pltpu.VMEM((count, count), jnp.float32)] * 2)
            + [pltpu.VMEM((18, 8, count), jnp.float32)],
            cost_estimate=pl.CostEstimate(
                flops=200 * len(panel_range) * count**3,
                bytes_accessed=4 * count * count,
                transcendentals=count,
            ),
            compiler_params=room(6),
            name="invert",
        )(*sources)

    by = {0: observed, 1: swap(observed, 1)}
    by.update({group: swap(observed, bit) for bit, group in ((2, 2), (4, 4), (8, 6))})
    panels, early = count // 8, 13 * count // 128
    midway = invert(range(early), (cross_order, diagonal, *levels))
    arrived, midway = lax.optimization_barrier(([by[g] for g in (2, 4, 6)], midway))
    for group, piece in zip((2, 4, 6), arrived):
        by[group] = piece
        by[group + 1] = swap(piece, 1)
    inverse, gains = invert(range(early, panels), (*midway, *(by[g] for g in (0, 2, 4, 6))))
    flips = (0, 2, 4, 6, 1, 3, 5, 7)
    return pl.pallas_call(
        functools.partial(update_kernel, width, flips),
        out_shape=jax.ShapeDtypeStruct(slab.shape, jnp.bfloat16),
        in_specs=[VMEM] * 8,
        out_specs=HBM,
        scratch_shapes=[
            pltpu.VMEM((len(flips), rows, width), jnp.bfloat16),
            pltpu.SemaphoreType.DMA((len(flips),)),
        ],
        compiler_params=room(12),
        name="update",
    )(inverse, gains, cross, slab, *(by[g] for g in (1, 3, 5, 7)))


def solution(mesh):
    plane = mesh.shape["cols"] == 1 and mesh.shape["rows"] == 4 * PLANE
    return jax.shard_map(
        plane_body if plane else general_body,
        mesh=mesh,
        in_specs=(P("rows", "cols"), P("rows", "cols"), P(), P()),
        out_specs=P("rows", "cols"),
        check_vma=False,
    )
```

```python
import functools

import jax
import jax.numpy as jnp
from jax import lax
from jax.experimental import pallas as pl
from jax.experimental.pallas import tpu as pltpu
from jax.sharding import PartitionSpec as P

CAP = 12
SLOTS = 16
PLANE = 8
PARTS = 3
VMEM = pl.BlockSpec(memory_space=pltpu.VMEM)
HBM = pl.BlockSpec(memory_space=pltpu.HBM)
MIB = 1 << 20


def room(mib):
    return pltpu.CompilerParams(vmem_limit_bytes=mib * MIB)


def dot32(a, b):
    return jnp.dot(a, b, preferred_element_type=jnp.float32)


def solve_gain(factor, right_side):
    forward = lax.linalg.triangular_solve(factor, right_side, left_side=True, lower=True)
    return lax.linalg.triangular_solve(
        factor, forward, left_side=True, lower=True, transpose_a=True
    )


def make_factor(picked_half, noise):
    picked = lax.all_gather(picked_half, "cols", axis=1, tiled=True).astype(jnp.float32)
    innovation = 0.5 * (picked + picked.T) + jnp.diag(noise)
    return jnp.linalg.cholesky(innovation)


def general_body(slab, cross, obs_index, noise):
    row_count = slab.shape[0]
    groups = lax.axis_size("rows")
    owners = obs_index // row_count
    local_row = obs_index % row_count
    owner_hit = (owners[:, None] == jnp.arange(groups, dtype=jnp.int32)[None, :]).astype(jnp.int32)
    before = jnp.cumsum(owner_hit, axis=0) - owner_hit
    slot_rank = jnp.sum(before * owner_hit, axis=1)
    mine = owners == lax.axis_index("rows")
    slot_hit = (
        mine[:, None] & (slot_rank[:, None] == jnp.arange(CAP, dtype=jnp.int32)[None, :])
    ).astype(jnp.bfloat16)
    row_hit = (local_row[:, None] == jnp.arange(row_count, dtype=jnp.int32)[None, :]).astype(
        jnp.bfloat16
    )
    selector = dot32(slot_hit.T, row_hit).astype(jnp.bfloat16)
    packed_cross = dot32(selector, cross).astype(jnp.bfloat16)
    packed_slab = dot32(selector, slab).astype(jnp.bfloat16)
    placed = owners * CAP + slot_rank
    all_cross, all_slab = (
        lax.all_gather(packed_cross, "rows", axis=0, tiled=True),
        lax.all_gather(packed_slab, "rows", axis=0, tiled=True),
    )
    factor = make_factor(all_cross[placed], noise)
    observed = all_slab[placed].astype(jnp.float32)
    gain = solve_gain(factor, observed).astype(jnp.bfloat16)
    update = dot32(lax.all_gather(cross, "cols", axis=1, tiled=True), gain)
    return (slab.astype(jnp.float32) - update).astype(jnp.bfloat16)


def spread_index(obs_ref, rows):
    count = obs_ref.shape[1]
    along = jnp.broadcast_to(obs_ref[...], (count, count))
    down = along.astype(jnp.float32).T.astype(jnp.int32)
    earlier_row = lax.broadcasted_iota(jnp.int32, (count, count), 0)
    earlier_col = lax.broadcasted_iota(jnp.int32, (count, count), 1)
    same = along // rows == down // rows
    rank_along = jnp.sum(
        jnp.where(same & (earlier_row < earlier_col), 1.0, 0.0), axis=0, keepdims=True
    ).astype(jnp.int32)
    rank_down = jnp.sum(
        jnp.where(same & (earlier_col < earlier_row), 1.0, 0.0), axis=1, keepdims=True
    ).astype(jnp.int32)
    return along, down, rank_along, rank_down


def column_group(device):
    return (device % PLANE) ^ (6 * ((device // PLANE) % 2))


def pick_kernel(
    groups, width, obs_hbm, slab_hbm, cross_hbm, out_hbm, picked_hbm, obs_ref, slab, cross, out, picked, sem, out_sem
):
    rows, count = slab.shape[0], obs_ref.shape[1]
    half = slab.shape[1] // 2

    def fetch(source, target, index):
        copy = pltpu.make_async_copy(source, target, sem.at[index])
        copy.start()
        return copy

    got_obs = fetch(obs_hbm, obs_ref, 0)
    got_cross = fetch(cross_hbm, cross, 1)
    got_slab = [
        fetch(slab_hbm.at[:, i * half : (i + 1) * half], slab.at[:, i * half : (i + 1) * half], 2 + i)
        for i in range(2)
    ]
    me = lax.axis_index("rows")
    got_obs.wait()
    along, down, rank, _ = spread_index(obs_ref, rows)
    picks = 4 * SLOTS
    slot = lax.broadcasted_iota(jnp.int32, (picks, count), 0)
    within, part = slot % SLOTS, slot // SLOTS
    wanted = jnp.where(
        part == 0,
        jnp.where(within < CAP, within, -1),
        jnp.where(within >= CAP, 4 * (part - 1) + within - CAP, -1),
    )
    mine = (along[:1] // rows) == me
    hit = jnp.where(mine & (rank == wanted), 1.0, 0.0).astype(jnp.bfloat16)
    local = lax.broadcasted_iota(jnp.int32, (count, rows), 1) == down[:, :rows] % rows
    selector = dot32(hit, jnp.where(local, 1.0, 0.0).astype(jnp.bfloat16)).astype(jnp.bfloat16)
    got_cross.wait()
    picked[...] = dot32(selector[:SLOTS], cross[...]).astype(jnp.bfloat16)
    lanes = width // 4
    sent = [pltpu.make_async_copy(picked, picked_hbm, out_sem.at[0])]
    sent[0].start()
    for group in range(PLANE):
        if group % 4 == 0:
            got_slab[group // 4].wait()
        got = dot32(selector, slab[:, group * width : (group + 1) * width])
        tail = got[:, 3 * lanes :]
        out[group * SLOTS : (group + 1) * SLOTS, :] = jnp.concatenate(
            [
                (
                    got[:SLOTS, t * lanes : (t + 1) * lanes]
                    + tail[(t + 1) * SLOTS : (t + 2) * SLOTS]
                ).astype(jnp.bfloat16)
                for t in range(3)
            ],
            axis=1,
        )
        if group % 2:
            source = out.at[(group - 1) * SLOTS : (group + 1) * SLOTS]
            for level in range(groups // PLANE):
                to = (level * PLANE + column_group(level * PLANE + group - 1)) * SLOTS
                copy = pltpu.make_async_copy(
                    source, out_hbm.at[to : to + 2 * SLOTS], out_sem.at[len(sent)]
                )
                copy.start()
                sent.append(copy)
    for copy in sent:
        copy.wait()


def order_kernel(rows, obs_ref, noise_ref, order_ref, cross_order_ref, diagonal_ref):
    count, slots = obs_ref.shape[1], order_ref.shape[1]
    _, down, _, rank = spread_index(obs_ref, rows)
    owner = down[:, :1] // rows
    lane = lax.broadcasted_iota(jnp.int32, (count, slots), 1)
    within, device = lane % SLOTS, lane // SLOTS

    def one_hot(hit):
        return jnp.where(hit, 1.0, 0.0).astype(jnp.bfloat16)

    owned = owner == device
    order_ref[:count, :] = one_hot(owned & (rank == within))
    for t in range(3):
        hit = (within >= CAP) & (rank == within + (4 * t - CAP))
        order_ref[(t + 1) * count : (t + 2) * count, :] = one_hot(owned & hit)
    apart = owner ^ lax.axis_index("rows")
    cross_order_ref[...] = one_hot((apart == device) & (rank == within))
    square = (count, count)
    on = lax.broadcasted_iota(jnp.int32, square, 0) == lax.broadcasted_iota(jnp.int32, square, 1)
    diagonal_ref[...] = jnp.where(on, noise_ref[...], 0.0)


def compact_kernel(order_ref, got_ref, observed_ref):
    count = observed_ref.shape[0]
    lanes = got_ref.shape[1] // 3
    head = dot32(order_ref[:count, :], got_ref[...])
    tail = jnp.zeros((count, lanes), jnp.float32)
    for t in range(3):
        hit = order_ref[(t + 1) * count : (t + 2) * count, :]
        tail += dot32(hit, got_ref[:, t * lanes : (t + 1) * lanes])
    observed_ref[:, : 3 * lanes] = head.astype(jnp.bfloat16)
    observed_ref[:, 3 * lanes :] = tail.astype(jnp.bfloat16)


def innovation_of(order_ref, diagonal_ref, *pieces):
    span = pieces[0].shape[0]
    picked = sum(
        dot32(order_ref[:, i * span : (i + 1) * span], piece[...])
        for i, piece in enumerate(pieces)
    )
    return 0.5 * (picked + picked.T) + diagonal_ref[...]


def tree_sum(terms):
    while len(terms) > 1:
        terms = [x + y for x, y in zip(terms[::2], terms[1::2])]
    return terms[0]


def sweep(e, step):
    def at(i, k):
        return max(i, k), min(i, k)

    for k in range(0, step, 2):
        a, b, c = e[k, k], e[k + 1, k], e[k + 1, k + 1]
        over = 1.0 / (a * c - b * b)
        pa, pb, pc = c * over, -b * over, a * over
        others = [i for i in range(step) if i not in (k, k + 1)]
        u = {i: e[at(i, k)] for i in others}
        v = {i: e[at(i, k + 1)] for i in others}
        su = {i: u[i] * pa + v[i] * pb for i in others}
        sv = {i: u[i] * pb + v[i] * pc for i in others}
        for i in others:
            for j in others:
                if j <= i:
                    e[i, j] = e[i, j] - (su[i] * u[j] + sv[i] * v[j])
        for i in others:
            e[at(i, k)], e[at(i, k + 1)] = su[i], sv[i]
        e[k, k], e[k + 1, k], e[k + 1, k + 1] = -pa, -pb, -pc


def gain_of(inverse_parts, observed):
    return dot32(inverse_parts, jnp.concatenate([observed] * PARTS, axis=0)).astype(jnp.bfloat16)


def invert_kernel(panel_range, sources, *refs):
    inputs, outputs, (spread_ref,) = refs[:sources], refs[sources:-1], refs[-1:]
    step = 8
    first, stop = panel_range[0], panel_range[-1] + 1
    if first == 0:
        inn = innovation_of(*inputs)
        state_ref, solved_ref = outputs
        size = inn.shape[0]
        state_ref[...] = inn
        given = state_ref
    else:
        given, solved_before = inputs[:2]
        out_ref, gain_ref, state_ref, solved_ref = outputs
        size = given.shape[0]
        done = first * step
        state_ref[:done, :] = given[:done, :]
        solved_ref[:done, :] = solved_before[:done, :]
    full, panels = (step, size), size // step
    m = {i: given[i * step : (i + 1) * step, :] for i in range(first, panels)}
    sub = lax.broadcasted_iota(jnp.int32, full, 0)
    lane = lax.broadcasted_iota(jnp.int32, full, 1)
    for p in panel_range:
        at, base = p * step, (p % 2) * (step + 1)
        row = m[p]
        for k in range(step):
            spread_ref[base + k] = jnp.broadcast_to(row[:, at + k : at + k + 1], full)
        e = {
            (i, k): jnp.broadcast_to(spread_ref[base + k, i : i + 1, :], full)
            for i in range(step)
            for k in range(i + 1)
        }
        inside = (lane >= at) & (lane < at + step)
        known = lane < at + step
        unit = jnp.where(inside, jnp.where(lane == sub + at, 1.0, 0.0), row)
        spread_ref[base + step] = unit
        sweep(e, step)
        rows_b = [
            jnp.broadcast_to(spread_ref[base + step, k : k + 1, :], full) for k in range(step)
        ]
        q = [
            tree_sum([e[max(i, k), min(i, k)] * rows_b[k] for k in range(step)])
            for i in range(step)
        ]
        for i in range(p + 1, panels):
            terms = [
                jnp.broadcast_to(m[i][:, at + k : at + k + 1], full) * q[k] for k in range(step)
            ]
            m[i] = jnp.where(inside, 0.0, m[i]) + tree_sum(terms)
        solved = q[0]
        for i in range(1, step):
            solved = jnp.where(sub == i, q[i], solved)
        state_ref[at : at + step, :] = jnp.where(known, unit, 0.0)
        solved_ref[at : at + step, :] = jnp.where(known, -solved, 0.0)
    if stop < panels:
        for i in range(stop, panels):
            state_ref[i * step : (i + 1) * step, :] = m[i]
        solved_ref[stop * step :, :] = jnp.zeros((size - stop * step, size), jnp.float32)
        return
    x = lax.dot_general(
        state_ref[...],
        solved_ref[...],
        (((0,), (0,)), ((), ())),
        precision=lax.Precision.HIGHEST,
        preferred_element_type=jnp.float32,
    )
    parts = []
    for part in range(PARTS):
        piece = x.astype(jnp.bfloat16)
        out_ref[part * size : (part + 1) * size, :] = piece
        x = x - piece.astype(jnp.float32)
        parts.append(piece)
    for index, piece in enumerate(inputs[2:]):
        gain_ref[index] = gain_of(jnp.concatenate(parts, axis=1), piece[...])


def update_kernel(width, flips, inverse_ref, gain_ref, cross_ref, slab_ref, *refs):
    pieces, (out_ref, held, sem) = refs[:-3], refs[-3:]
    place = column_group(lax.axis_index("rows"))
    cross = cross_ref[...]
    size = cross.shape[1]
    inverse = jnp.concatenate(
        [inverse_ref[t * size : (t + 1) * size] for t in range(PARTS)], axis=1
    )
    copies = []
    ready = gain_ref.shape[0]
    gains = [gain_ref[i] for i in range(ready)]
    for index, flip in enumerate(flips):
        if index == ready:
            gains += [gain_of(inverse, piece[...]) for piece in pieces]
        at = pl.multiple_of((place ^ flip) * width, width)
        new = slab_ref[:, pl.ds(at, width)].astype(jnp.float32) - dot32(cross, gains[index])
        held[index] = new.astype(jnp.bfloat16)
        copy = pltpu.make_async_copy(
            held.at[index], out_ref.at[:, pl.ds(at, width)], sem.at[index]
        )
        copy.start()
        copies.append(copy)
    for copy in copies:
        copy.wait()


def plane_body(slab, cross, obs_index, noise):
    groups = lax.axis_size("rows")
    rows, columns = slab.shape
    count = cross.shape[1]
    width = columns // PLANE
    obs = obs_index.reshape(1, count)
    packed, picked = pl.pallas_call(
        functools.partial(pick_kernel, groups, width),
        out_shape=(
            jax.ShapeDtypeStruct((groups * SLOTS, 3 * width // 4), jnp.bfloat16),
            jax.ShapeDtypeStruct((SLOTS, count), jnp.bfloat16),
        ),
        in_specs=[HBM] * 3,
        out_specs=(HBM, HBM),
        scratch_shapes=[
            pltpu.VMEM((1, count), jnp.int32),
            pltpu.VMEM(slab.shape, jnp.bfloat16),
            pltpu.VMEM(cross.shape, jnp.bfloat16),
            pltpu.VMEM((PLANE * SLOTS, 3 * width // 4), jnp.bfloat16),
            pltpu.VMEM((SLOTS, count), jnp.bfloat16),
            pltpu.SemaphoreType.DMA((4,)),
            pltpu.SemaphoreType.DMA((1 + groups // 2,)),
        ],
        compiler_params=room(56),
        name="pick",
    )(obs, slab, cross)
    order, cross_order, diagonal = pl.pallas_call(
        functools.partial(order_kernel, rows),
        out_shape=(
            jax.ShapeDtypeStruct((4 * count, groups * SLOTS), jnp.bfloat16),
            jax.ShapeDtypeStruct((count, groups * SLOTS), jnp.bfloat16),
            jax.ShapeDtypeStruct((count, count), jnp.float32),
        ),
        in_specs=[VMEM] * 2,
        out_specs=(VMEM,) * 3,
        cost_estimate=pl.CostEstimate(
            flops=1000 * count**3, bytes_accessed=4 * count * count, transcendentals=0
        ),
        compiler_params=room(8),
        name="order",
    )(obs, noise.reshape(1, count))

    def swap(value, bit):
        return lax.ppermute(value, "rows", [(i, i ^ bit) for i in range(groups)])

    got = lax.all_to_all(
        packed.reshape(groups, SLOTS, -1), "rows", split_axis=0, concat_axis=0, tiled=True
    ).reshape(groups * SLOTS, -1)
    chip = jnp.concatenate([picked, swap(picked, 1)])
    plane = jnp.concatenate([chip] + [swap(chip, bits) for bits in (2, 4, 6)])
    levels = [plane] + [swap(plane, bits) for bits in range(PLANE, groups, PLANE)]
    observed = pl.pallas_call(
        compact_kernel,
        out_shape=jax.ShapeDtypeStruct((count, width), jnp.bfloat16),
        in_specs=[VMEM] * 2,
        out_specs=VMEM,
        compiler_params=room(8),
        name="compact",
    )(order, got)
    square = jax.ShapeDtypeStruct((count, count), jnp.float32)

    def invert(panel_range, sources):
        first = panel_range[0] == 0
        parts = jax.ShapeDtypeStruct((PARTS * count, count), jnp.bfloat16)
        gains = jax.ShapeDtypeStruct((len(sources) - 2, count, width), jnp.bfloat16)
        return pl.pallas_call(
            functools.partial(invert_kernel, panel_range, len(sources)),
            out_shape=(square, square) if first else (parts, gains),
            in_specs=[VMEM] * len(sources),
            out_specs=(VMEM, VMEM),
            scratch_shapes=([] if first else [pltpu.VMEM((count, count), jnp.float32)] * 2)
            + [pltpu.VMEM((18, 8, count), jnp.float32)],
            cost_estimate=pl.CostEstimate(
                flops=200 * len(panel_range) * count**3,
                bytes_accessed=4 * count * count,
                transcendentals=count,
            ),
            compiler_params=room(6),
            name="invert",
        )(*sources)

    by = {0: observed, 1: swap(observed, 1)}
    by.update({group: swap(observed, bit) for bit, group in ((2, 2), (4, 4), (8, 6))})
    panels, early = count // 8, 13 * count // 128
    midway = invert(range(early), (cross_order, diagonal, *levels))
    arrived, midway = lax.optimization_barrier(([by[g] for g in (2, 4, 6)], midway))
    for group, piece in zip((2, 4, 6), arrived):
        by[group] = piece
        by[group + 1] = swap(piece, 1)
    inverse, gains = invert(range(early, panels), (*midway, *(by[g] for g in (0, 1, 2, 4, 6))))
    flips = (0, 1, 2, 4, 6, 3, 5, 7)
    return pl.pallas_call(
        functools.partial(update_kernel, width, flips),
        out_shape=jax.ShapeDtypeStruct(slab.shape, jnp.bfloat16),
        in_specs=[VMEM] * 7,
        out_specs=HBM,
        scratch_shapes=[
            pltpu.VMEM((len(flips), rows, width), jnp.bfloat16),
            pltpu.SemaphoreType.DMA((len(flips),)),
        ],
        compiler_params=room(12),
        name="update",
    )(inverse, gains, cross, slab, *(by[g] for g in (3, 5, 7)))


def solution(mesh):
    plane = mesh.shape["cols"] == 1 and mesh.shape["rows"] == 4 * PLANE
    return jax.shard_map(
        plane_body if plane else general_body,
        mesh=mesh,
        in_specs=(P("rows", "cols"), P("rows", "cols"), P(), P()),
        out_specs=P("rows", "cols"),
        check_vma=False,
    )
```

```python
import functools

import jax
import jax.numpy as jnp
from jax import lax
from jax.experimental import pallas as pl
from jax.experimental.pallas import tpu as pltpu
from jax.sharding import PartitionSpec as P

CAP = 12
SLOTS = 16
PLANE = 8
PARTS = 3
VMEM = pl.BlockSpec(memory_space=pltpu.VMEM)
HBM = pl.BlockSpec(memory_space=pltpu.HBM)
MIB = 1 << 20


def room(mib):
    return pltpu.CompilerParams(vmem_limit_bytes=mib * MIB)


def dot32(a, b):
    return jnp.dot(a, b, preferred_element_type=jnp.float32)


def solve_gain(factor, right_side):
    forward = lax.linalg.triangular_solve(factor, right_side, left_side=True, lower=True)
    return lax.linalg.triangular_solve(
        factor, forward, left_side=True, lower=True, transpose_a=True
    )


def make_factor(picked_half, noise):
    picked = lax.all_gather(picked_half, "cols", axis=1, tiled=True).astype(jnp.float32)
    innovation = 0.5 * (picked + picked.T) + jnp.diag(noise)
    return jnp.linalg.cholesky(innovation)


def general_body(slab, cross, obs_index, noise):
    row_count = slab.shape[0]
    groups = lax.axis_size("rows")
    owners = obs_index // row_count
    local_row = obs_index % row_count
    owner_hit = (owners[:, None] == jnp.arange(groups, dtype=jnp.int32)[None, :]).astype(jnp.int32)
    before = jnp.cumsum(owner_hit, axis=0) - owner_hit
    slot_rank = jnp.sum(before * owner_hit, axis=1)
    mine = owners == lax.axis_index("rows")
    slot_hit = (
        mine[:, None] & (slot_rank[:, None] == jnp.arange(CAP, dtype=jnp.int32)[None, :])
    ).astype(jnp.bfloat16)
    row_hit = (local_row[:, None] == jnp.arange(row_count, dtype=jnp.int32)[None, :]).astype(
        jnp.bfloat16
    )
    selector = dot32(slot_hit.T, row_hit).astype(jnp.bfloat16)
    packed_cross = dot32(selector, cross).astype(jnp.bfloat16)
    packed_slab = dot32(selector, slab).astype(jnp.bfloat16)
    placed = owners * CAP + slot_rank
    all_cross, all_slab = (
        lax.all_gather(packed_cross, "rows", axis=0, tiled=True),
        lax.all_gather(packed_slab, "rows", axis=0, tiled=True),
    )
    factor = make_factor(all_cross[placed], noise)
    observed = all_slab[placed].astype(jnp.float32)
    gain = solve_gain(factor, observed).astype(jnp.bfloat16)
    update = dot32(lax.all_gather(cross, "cols", axis=1, tiled=True), gain)
    return (slab.astype(jnp.float32) - update).astype(jnp.bfloat16)


def spread_index(obs_ref, rows):
    count = obs_ref.shape[1]
    along = jnp.broadcast_to(obs_ref[...], (count, count))
    down = along.astype(jnp.float32).T.astype(jnp.int32)
    earlier_row = lax.broadcasted_iota(jnp.int32, (count, count), 0)
    earlier_col = lax.broadcasted_iota(jnp.int32, (count, count), 1)
    same = along // rows == down // rows
    rank_along = jnp.sum(
        jnp.where(same & (earlier_row < earlier_col), 1.0, 0.0), axis=0, keepdims=True
    ).astype(jnp.int32)
    rank_down = jnp.sum(
        jnp.where(same & (earlier_col < earlier_row), 1.0, 0.0), axis=1, keepdims=True
    ).astype(jnp.int32)
    return along, down, rank_along, rank_down


def column_group(device):
    return (device % PLANE) ^ (6 * ((device // PLANE) % 2))


def pick_kernel(
    groups, width, obs_hbm, slab_hbm, cross_hbm, out_hbm, picked_hbm, obs_ref, slab, cross, out, picked, sem, out_sem
):
    rows, count = slab.shape[0], obs_ref.shape[1]
    half = slab.shape[1] // 2

    def fetch(source, target, index):
        copy = pltpu.make_async_copy(source, target, sem.at[index])
        copy.start()
        return copy

    got_obs = fetch(obs_hbm, obs_ref, 0)
    got_cross = fetch(cross_hbm, cross, 1)
    got_slab = [
        fetch(slab_hbm.at[:, i * half : (i + 1) * half], slab.at[:, i * half : (i + 1) * half], 2 + i)
        for i in range(2)
    ]
    me = lax.axis_index("rows")
    got_obs.wait()
    along, down, rank, _ = spread_index(obs_ref, rows)
    picks = 4 * SLOTS
    slot = lax.broadcasted_iota(jnp.int32, (picks, count), 0)
    within, part = slot % SLOTS, slot // SLOTS
    wanted = jnp.where(
        part == 0,
        jnp.where(within < CAP, within, -1),
        jnp.where(within >= CAP, 4 * (part - 1) + within - CAP, -1),
    )
    mine = (along[:1] // rows) == me
    hit = jnp.where(mine & (rank == wanted), 1.0, 0.0).astype(jnp.bfloat16)
    local = lax.broadcasted_iota(jnp.int32, (count, rows), 1) == down[:, :rows] % rows
    selector = dot32(hit, jnp.where(local, 1.0, 0.0).astype(jnp.bfloat16)).astype(jnp.bfloat16)
    got_cross.wait()
    picked[...] = dot32(selector[:SLOTS], cross[...]).astype(jnp.bfloat16)
    lanes = width // 4
    sent = [pltpu.make_async_copy(picked, picked_hbm, out_sem.at[0])]
    sent[0].start()
    for group in range(PLANE):
        if group % 4 == 0:
            got_slab[group // 4].wait()
        got = dot32(selector, slab[:, group * width : (group + 1) * width])
        tail = got[:, 3 * lanes :]
        out[group * SLOTS : (group + 1) * SLOTS, :] = jnp.concatenate(
            [
                (
                    got[:SLOTS, t * lanes : (t + 1) * lanes]
                    + tail[(t + 1) * SLOTS : (t + 2) * SLOTS]
                ).astype(jnp.bfloat16)
                for t in range(3)
            ],
            axis=1,
        )
        if group % 2:
            source = out.at[(group - 1) * SLOTS : (group + 1) * SLOTS]
            for level in range(groups // PLANE):
                to = (level * PLANE + column_group(level * PLANE + group - 1)) * SLOTS
                copy = pltpu.make_async_copy(
                    source, out_hbm.at[to : to + 2 * SLOTS], out_sem.at[len(sent)]
                )
                copy.start()
                sent.append(copy)
    for copy in sent:
        copy.wait()


def order_kernel(rows, obs_ref, noise_ref, order_ref, cross_order_ref, diagonal_ref):
    count, slots = obs_ref.shape[1], order_ref.shape[1]
    _, down, _, rank = spread_index(obs_ref, rows)
    owner = down[:, :1] // rows
    lane = lax.broadcasted_iota(jnp.int32, (count, slots), 1)
    within, device = lane % SLOTS, lane // SLOTS

    def one_hot(hit):
        return jnp.where(hit, 1.0, 0.0).astype(jnp.bfloat16)

    owned = owner == device
    order_ref[:count, :] = one_hot(owned & (rank == within))
    for t in range(3):
        hit = (within >= CAP) & (rank == within + (4 * t - CAP))
        order_ref[(t + 1) * count : (t + 2) * count, :] = one_hot(owned & hit)
    apart = owner ^ lax.axis_index("rows")
    cross_order_ref[...] = one_hot((apart == device) & (rank == within))
    square = (count, count)
    on = lax.broadcasted_iota(jnp.int32, square, 0) == lax.broadcasted_iota(jnp.int32, square, 1)
    diagonal_ref[...] = jnp.where(on, noise_ref[...], 0.0)


def compact_kernel(order_ref, got_ref, observed_ref):
    count = observed_ref.shape[0]
    lanes = got_ref.shape[1] // 3
    head = dot32(order_ref[:count, :], got_ref[...])
    tail = jnp.zeros((count, lanes), jnp.float32)
    for t in range(3):
        hit = order_ref[(t + 1) * count : (t + 2) * count, :]
        tail += dot32(hit, got_ref[:, t * lanes : (t + 1) * lanes])
    observed_ref[:, : 3 * lanes] = head.astype(jnp.bfloat16)
    observed_ref[:, 3 * lanes :] = tail.astype(jnp.bfloat16)


def innovation_of(order_ref, diagonal_ref, *pieces):
    span = pieces[0].shape[0]
    picked = sum(
        dot32(order_ref[:, i * span : (i + 1) * span], piece[...])
        for i, piece in enumerate(pieces)
    )
    return 0.5 * (picked + picked.T) + diagonal_ref[...]


def tree_sum(terms):
    while len(terms) > 1:
        terms = [x + y for x, y in zip(terms[::2], terms[1::2])]
    return terms[0]


def sweep(e, step):
    def at(i, k):
        return max(i, k), min(i, k)

    for k in range(0, step, 2):
        a, b, c = e[k, k], e[k + 1, k], e[k + 1, k + 1]
        over = 1.0 / (a * c - b * b)
        pa, pb, pc = c * over, -b * over, a * over
        others = [i for i in range(step) if i not in (k, k + 1)]
        u = {i: e[at(i, k)] for i in others}
        v = {i: e[at(i, k + 1)] for i in others}
        su = {i: u[i] * pa + v[i] * pb for i in others}
        sv = {i: u[i] * pb + v[i] * pc for i in others}
        for i in others:
            for j in others:
                if j <= i:
                    e[i, j] = e[i, j] - (su[i] * u[j] + sv[i] * v[j])
        for i in others:
            e[at(i, k)], e[at(i, k + 1)] = su[i], sv[i]
        e[k, k], e[k + 1, k], e[k + 1, k + 1] = -pa, -pb, -pc


def gain_of(inverse_parts, observed):
    return dot32(inverse_parts, jnp.concatenate([observed] * PARTS, axis=0)).astype(jnp.bfloat16)


def invert_kernel(panel_range, sources, *refs):
    inputs, outputs, (spread_ref,) = refs[:sources], refs[sources:-1], refs[-1:]
    step = 8
    first, stop = panel_range[0], panel_range[-1] + 1
    if first == 0:
        inn = innovation_of(*inputs)
        state_ref, solved_ref = outputs
        size = inn.shape[0]
        state_ref[...] = inn
        given = state_ref
    else:
        given, solved_before = inputs[:2]
        out_ref, gain_ref, state_ref, solved_ref = outputs
        size = given.shape[0]
        done = first * step
        state_ref[:done, :] = given[:done, :]
        solved_ref[:done, :] = solved_before[:done, :]
    full, panels = (step, size), size // step
    m = {i: given[i * step : (i + 1) * step, :] for i in range(first, panels)}
    sub = lax.broadcasted_iota(jnp.int32, full, 0)
    lane = lax.broadcasted_iota(jnp.int32, full, 1)
    for p in panel_range:
        at, base = p * step, (p % 2) * (step + 1)
        row = m[p]
        for k in range(step):
            spread_ref[base + k] = jnp.broadcast_to(row[:, at + k : at + k + 1], full)
        e = {
            (i, k): jnp.broadcast_to(spread_ref[base + k, i : i + 1, :], full)
            for i in range(step)
            for k in range(i + 1)
        }
        inside = (lane >= at) & (lane < at + step)
        known = lane < at + step
        unit = jnp.where(inside, jnp.where(lane == sub + at, 1.0, 0.0), row)
        spread_ref[base + step] = unit
        sweep(e, step)
        rows_b = [
            jnp.broadcast_to(spread_ref[base + step, k : k + 1, :], full) for k in range(step)
        ]
        q = [
            tree_sum([e[max(i, k), min(i, k)] * rows_b[k] for k in range(step)])
            for i in range(step)
        ]
        for i in range(p + 1, panels):
            terms = [
                jnp.broadcast_to(m[i][:, at + k : at + k + 1], full) * q[k] for k in range(step)
            ]
            m[i] = jnp.where(inside, 0.0, m[i]) + tree_sum(terms)
        solved = q[0]
        for i in range(1, step):
            solved = jnp.where(sub == i, q[i], solved)
        state_ref[at : at + step, :] = jnp.where(known, unit, 0.0)
        solved_ref[at : at + step, :] = jnp.where(known, -solved, 0.0)
    if stop < panels:
        for i in range(stop, panels):
            state_ref[i * step : (i + 1) * step, :] = m[i]
        solved_ref[stop * step :, :] = jnp.zeros((size - stop * step, size), jnp.float32)
        return
    x = lax.dot_general(
        state_ref[...],
        solved_ref[...],
        (((0,), (0,)), ((), ())),
        precision=lax.Precision.HIGHEST,
        preferred_element_type=jnp.float32,
    )
    parts = []
    for part in range(PARTS):
        piece = x.astype(jnp.bfloat16)
        out_ref[part * size : (part + 1) * size, :] = piece
        x = x - piece.astype(jnp.float32)
        parts.append(piece)
    for index, piece in enumerate(inputs[2:]):
        gain_ref[index] = gain_of(jnp.concatenate(parts, axis=1), piece[...])


def update_kernel(width, flips, inverse_ref, gain_ref, cross_ref, slab_ref, *refs):
    pieces, (out_ref, held, sem) = refs[:-3], refs[-3:]
    place = column_group(lax.axis_index("rows"))
    cross = cross_ref[...]
    size = cross.shape[1]
    inverse = jnp.concatenate(
        [inverse_ref[t * size : (t + 1) * size] for t in range(PARTS)], axis=1
    )
    copies = []
    ready = gain_ref.shape[0]
    gains = [gain_ref[i] for i in range(ready)]
    for index, flip in enumerate(flips):
        if index == ready:
            gains += [gain_of(inverse, piece[...]) for piece in pieces]
        at = pl.multiple_of((place ^ flip) * width, width)
        new = slab_ref[:, pl.ds(at, width)].astype(jnp.float32) - dot32(cross, gains[index])
        held[index] = new.astype(jnp.bfloat16)
        copy = pltpu.make_async_copy(
            held.at[index], out_ref.at[:, pl.ds(at, width)], sem.at[index]
        )
        copy.start()
        copies.append(copy)
    for copy in copies:
        copy.wait()


def plane_body(slab, cross, obs_index, noise):
    groups = lax.axis_size("rows")
    rows, columns = slab.shape
    count = cross.shape[1]
    width = columns // PLANE
    obs = obs_index.reshape(1, count)
    packed, picked = pl.pallas_call(
        functools.partial(pick_kernel, groups, width),
        out_shape=(
            jax.ShapeDtypeStruct((groups * SLOTS, 3 * width // 4), jnp.bfloat16),
            jax.ShapeDtypeStruct((SLOTS, count), jnp.bfloat16),
        ),
        in_specs=[HBM] * 3,
        out_specs=(HBM, HBM),
        scratch_shapes=[
            pltpu.VMEM((1, count), jnp.int32),
            pltpu.VMEM(slab.shape, jnp.bfloat16),
            pltpu.VMEM(cross.shape, jnp.bfloat16),
            pltpu.VMEM((PLANE * SLOTS, 3 * width // 4), jnp.bfloat16),
            pltpu.VMEM((SLOTS, count), jnp.bfloat16),
            pltpu.SemaphoreType.DMA((4,)),
            pltpu.SemaphoreType.DMA((1 + groups // 2,)),
        ],
        compiler_params=room(56),
        name="pick",
    )(obs, slab, cross)
    order, cross_order, diagonal = pl.pallas_call(
        functools.partial(order_kernel, rows),
        out_shape=(
            jax.ShapeDtypeStruct((4 * count, groups * SLOTS), jnp.bfloat16),
            jax.ShapeDtypeStruct((count, groups * SLOTS), jnp.bfloat16),
            jax.ShapeDtypeStruct((count, count), jnp.float32),
        ),
        in_specs=[VMEM] * 2,
        out_specs=(VMEM,) * 3,
        cost_estimate=pl.CostEstimate(
            flops=1000 * count**3, bytes_accessed=4 * count * count, transcendentals=0
        ),
        compiler_params=room(8),
        name="order",
    )(obs, noise.reshape(1, count))

    def swap(value, bit):
        return lax.ppermute(value, "rows", [(i, i ^ bit) for i in range(groups)])

    got = lax.all_to_all(
        packed.reshape(groups, SLOTS, -1), "rows", split_axis=0, concat_axis=0, tiled=True
    ).reshape(groups * SLOTS, -1)
    chip = jnp.concatenate([picked, swap(picked, 1)])
    plane = jnp.concatenate([chip] + [swap(chip, bits) for bits in (2, 4, 6)])
    levels = [plane] + [swap(plane, bits) for bits in range(PLANE, groups, PLANE)]
    observed = pl.pallas_call(
        compact_kernel,
        out_shape=jax.ShapeDtypeStruct((count, width), jnp.bfloat16),
        in_specs=[VMEM] * 2,
        out_specs=VMEM,
        compiler_params=room(8),
        name="compact",
    )(order, got)
    square = jax.ShapeDtypeStruct((count, count), jnp.float32)

    def invert(panel_range, sources):
        first = panel_range[0] == 0
        parts = jax.ShapeDtypeStruct((PARTS * count, count), jnp.bfloat16)
        gains = jax.ShapeDtypeStruct((len(sources) - 2, count, width), jnp.bfloat16)
        return pl.pallas_call(
            functools.partial(invert_kernel, panel_range, len(sources)),
            out_shape=(square, square) if first else (parts, gains),
            in_specs=[VMEM] * len(sources),
            out_specs=(VMEM, VMEM),
            scratch_shapes=([] if first else [pltpu.VMEM((count, count), jnp.float32)] * 2)
            + [pltpu.VMEM((18, 8, count), jnp.float32)],
            cost_estimate=pl.CostEstimate(
                flops=200 * len(panel_range) * count**3,
                bytes_accessed=4 * count * count,
                transcendentals=count,
            ),
            compiler_params=room(6),
            name="invert",
        )(*sources)

    by = {0: observed, 1: swap(observed, 1)}
    by.update({group: swap(observed, bit) for bit, group in ((2, 2), (4, 4), (8, 6))})
    panels, early = count // 8, 14 * count // 128
    midway = invert(range(early), (cross_order, diagonal, *levels))
    arrived, midway = lax.optimization_barrier(([by[g] for g in (2, 4, 6)], midway))
    for group, piece in zip((2, 4, 6), arrived):
        by[group] = piece
        by[group + 1] = swap(piece, 1)
    inverse, gains = invert(range(early, panels), (*midway, *(by[g] for g in (0, 2, 4, 6))))
    flips = (0, 2, 4, 6, 1, 3, 5, 7)
    return pl.pallas_call(
        functools.partial(update_kernel, width, flips),
        out_shape=jax.ShapeDtypeStruct(slab.shape, jnp.bfloat16),
        in_specs=[VMEM] * 8,
        out_specs=HBM,
        scratch_shapes=[
            pltpu.VMEM((len(flips), rows, width), jnp.bfloat16),
            pltpu.SemaphoreType.DMA((len(flips),)),
        ],
        compiler_params=room(12),
        name="update",
    )(inverse, gains, cross, slab, *(by[g] for g in (1, 3, 5, 7)))


def solution(mesh):
    plane = mesh.shape["cols"] == 1 and mesh.shape["rows"] == 4 * PLANE
    return jax.shard_map(
        plane_body if plane else general_body,
        mesh=mesh,
        in_specs=(P("rows", "cols"), P("rows", "cols"), P(), P()),
        out_specs=P("rows", "cols"),
        check_vma=False,
    )
```
